128 devices in a mesh: front: 8 (over y_hi, x), row: 4 (over z), col: 4 (over y_lo, core).
Axes of the slice: x: 4, y: 4 (y_hi: 2, y_lo: 2; y = y_hi * 2 + y_lo), z: 4, core: 2. Of those that a mesh axis runs over, the one named last changes fastest.
Arguments:
- own_rows: float32 [8, 16384, 1024], P('front', 'row', 'col'), may hold values from -0.046875 to 0.046875
- child_blocks: float32 [8, 2, 2048, 1024], P('front', None, 'row', 'col'), may hold values from -0.125 to 0.125
- child_parent: int32 [8, 2], replicated, may hold values from 0 to 7
- child_live: int32 [8, 2], replicated, may hold values from 1 to 2048
- child_first: int32 [8, 2], replicated, may hold values from 0 to 15
Outputs:
- factor: float32 [8, 1024, 1024], P('front', 'row', 'col')
The draws below stay inside these ranges and needn't reach their ends.
All inputs are finite; a program needn't handle non-finite values.
Results may differ from the reference program's by a relative error of at most 0.00016.
Values sent between devices are 32-bit elements; how exact they have to be, the bound alone decides.
No kernel may reach another device: no remote copies, remote signals or barrier semaphores. Data moves between devices by JAX's collectives and lax.ppermute only.
A program may use at most 128 MiB of HBM per device.

```python
import math
import jax
import jax.numpy as jnp
import numpy as np
from jax import lax

FC = 1024
PANEL = 64
SLOTS = 2
OWN = 16384
CROWS = 2048
N_FRONT = 8


def plant(array, own_key, low, high):
    place = [jax.random.randint(jax.random.fold_in(own_key, axis), (), 0, length) for axis, length in enumerate(array.shape)]
    widest = array.shape.index(max(array.shape))
    beside = place[:widest] + [(place[widest] + 1) % array.shape[widest]] + place[widest + 1:]
    return array.at[tuple(place)].set(low).at[tuple(beside)].set(high)


def block_scale(own_key, shape, split, least, high):
    gain, own = 1.0, jax.random.fold_in(own_key, 6)
    for position, parts in split:
        steps = jnp.exp(jax.random.uniform(jax.random.fold_in(own, position), (parts,), jnp.float32, least / len(split), high / len(split)))
        gain = gain * jnp.repeat(steps, shape[position] // parts).reshape([-1 if axis == position else 1 for axis in range(len(shape))])
    return gain


def rank_table(count, slope):
    loads = [(1 << 20) // math.isqrt(grade ** slope) + 1 for grade in range(1, count + 1)]
    scale = 1 + sum(loads) // (1 << 30)
    return np.cumsum(np.array([max(1, weight // scale) for weight in loads]))


def ranked(rng, shape, amount, skew):
    table = rank_table(amount, skew)
    pick = jax.random.randint(jax.random.fold_in(rng, 1), shape, 0, int(table[amount - 1]))
    grade = jnp.searchsorted(jnp.asarray(table, jnp.int32), pick, side="right")
    return jax.random.permutation(jax.random.fold_in(rng, 2), amount)[grade].astype(jnp.int32)


def scatter_about(own_key, shape, scale, limit, pieces=(), kind=jnp.bfloat16):
    factor_of = block_scale(own_key, shape, pieces, -0.22, 0.18) if pieces else 1.0
    entries = jax.random.normal(own_key, shape, jnp.float32) * scale * factor_of
    return jnp.minimum(jnp.maximum(entries, -limit), limit).astype(kind)


def setup_inputs(seed: int = 0) -> dict:
    streams_of = jax.random.split(jax.random.key(seed), 6)
    return {
        "own_rows": scatter_about(streams_of[0], (N_FRONT, OWN, FC), OWN ** -0.5, 0.046875, ((0, 8), (1, 4), (2, 4)), jnp.float32),
        "child_blocks": scatter_about(streams_of[1], (N_FRONT, SLOTS, CROWS, FC), CROWS ** -0.5, 0.125, ((0, 8), (2, 4), (3, 4)), jnp.float32),
        "child_parent": plant(ranked(streams_of[2], (N_FRONT, SLOTS), N_FRONT, 2), jax.random.fold_in(streams_of[2], 3), 0, N_FRONT - 1).astype(jnp.int32),
        "child_live": plant(jax.random.randint(streams_of[3], (N_FRONT, SLOTS), 1, CROWS + 1), jax.random.fold_in(streams_of[3], 1), 1, CROWS).astype(jnp.int32),
        "child_first": plant(jax.random.randint(streams_of[4], (N_FRONT, SLOTS), 0, FC // PANEL), jax.random.fold_in(streams_of[4], 1), 0, (FC // PANEL) - 1).astype(jnp.int32),
    }


def child_gram(packed):
    block, keep_rows, keep_cols = packed
    masked = block * keep_rows[:, None] * keep_cols[None, :]
    return jnp.einsum('ik,il->kl', masked, masked, precision=lax.Precision.HIGHEST)

def reference(own_rows, child_blocks, child_parent, child_live, child_first):
    row_pos = jnp.arange(CROWS, dtype=jnp.int32)
    col_pos = jnp.arange(FC, dtype=jnp.int32)
    keep_rows = (row_pos[None, None, :] < child_live[:, :, None]).astype(jnp.float32)
    keep_cols = (col_pos[None, None, :] >= PANEL * child_first[:, :, None]).astype(jnp.float32)
    count = N_FRONT * SLOTS
    grams = lax.map(child_gram, (child_blocks.reshape(count, CROWS, FC), keep_rows.reshape(count, CROWS), keep_cols.reshape(count, FC)))
    onehot = (child_parent.reshape(count)[:, None] == jnp.arange(N_FRONT, dtype=jnp.int32)[None, :]).astype(jnp.float32)

    def one_front(packed):
        own, weights = packed
        gram_full = jnp.einsum('ik,il->kl', own, own, precision=lax.Precision.HIGHEST)
        gram_full = gram_full + jnp.einsum('k,kab->ab', weights, grams, precision=lax.Precision.HIGHEST)
        lower_factor = jnp.linalg.cholesky(gram_full)
        return lower_factor.T
    return lax.map(one_front, (own_rows, onehot.T))
```

```python
import jax
import jax.numpy as jnp
from jax import lax
from jax.experimental import pallas as pl
from jax.experimental.pallas import tpu as pltpu
from jax.sharding import PartitionSpec as P

PANEL = 64
NB = 128
SUB = 8
HI = lax.Precision.HIGHEST
CHUNKS = (1024, 768, 256)


def dot(x, y):
    return lax.dot_general(x, y, (((1,), (0,)), ((), ())), precision=HI, preferred_element_type=jnp.float32)


def tdot(x, y):
    return lax.dot_general(x, y, (((0,), (0,)), ((), ())), precision=HI, preferred_element_type=jnp.float32)


def spread(x):
    return jnp.broadcast_to(x, (SUB, NB))


def diag_factor(block):
    rows = lax.broadcasted_iota(jnp.int32, (SUB, NB), 0)
    lanes = lax.broadcasted_iota(jnp.int32, (SUB, NB), 1)
    count = NB // SUB
    a = [block[SUB * s : SUB * (s + 1), :] for s in range(count)]
    e = [jnp.where(lanes == rows + SUB * s, 1.0, 0.0) for s in range(count)]
    for s in range(count):
        left, right = a[s], e[s]
        cols = [spread(left[:, SUB * s + k : SUB * s + k + 1]) for k in range(SUB)]
        for k in range(SUB):
            rs = lax.rsqrt(cols[k][k : k + 1, :])
            m = jnp.where(rows > k, cols[k] * rs, 0.0)
            lrow = left[k : k + 1, :] * rs
            rrow = right[k : k + 1, :] * rs
            left = jnp.where(rows == k, lrow, left - m * lrow)
            right = jnp.where(rows == k, rrow, right - m * rrow)
            for l in range(k + 1, SUB):
                cols[l] = cols[l] - m * (cols[l][k : k + 1, :] * rs)
        left = jnp.where(lanes >= rows + SUB * s, left, 0.0)
        a[s], e[s] = left, right
        if s + 1 < count:
            turned = left.T
            lrows = [spread(left[k : k + 1, :]) for k in range(SUB)]
            rrows = [spread(right[k : k + 1, :]) for k in range(SUB)]
            for t in range(s + 1, count):
                for k in range(SUB):
                    mt = spread(turned[SUB * t : SUB * (t + 1), k : k + 1])
                    a[t] = a[t] - mt * lrows[k]
                    e[t] = e[t] - mt * rrows[k]
    return jnp.concatenate(a, 0), jnp.concatenate(e, 0)


def eliminate(work, size):
    blocks = size // NB

    def step(j, carry):
        here = pl.ds(pl.multiple_of(j * NB, NB), NB)
        r, m = diag_factor(work[here, here])
        work[here, :] = dot(m, work[here, :])
        work[here, here] = r

        def below(i, inner):
            there = pl.ds(pl.multiple_of(i * NB, NB), NB)
            work[there, :] = work[there, :] - tdot(work[here, there], work[here, :])
            return inner

        return lax.fori_loop(j + 1, blocks, below, carry)

    lax.fori_loop(0, blocks, step, 0)


def upper(x):
    return jnp.where(
        lax.broadcasted_iota(jnp.int32, x.shape, 1) >= lax.broadcasted_iota(jnp.int32, x.shape, 0), x, 0.0
    )


def place(ref, where, mine, other):
    ring, _, part, width = mine.shape
    r, k = where[0], where[1]
    for source, core in ((mine, k), (other, 1 - k)):
        for s in range(ring):
            q = lax.rem(r - s + ring, ring)
            at = pl.ds(pl.multiple_of(core * width + q * part, part), part)
            ref[at, pl.ds(pl.multiple_of(core * width, width), width)] = source[s, 0]
            ref[at, pl.ds(pl.multiple_of((1 - core) * width, width), width)] = source[s, 1]


def head_kernel(where, mine, other, r_ref, m_ref, work):
    n = r_ref.shape[0]
    place(work, where, mine, other)
    work[:, n:] = jnp.where(
        lax.broadcasted_iota(jnp.int32, (n, n), 1) == lax.broadcasted_iota(jnp.int32, (n, n), 0), 1.0, 0.0
    )
    eliminate(work, n)
    r_ref[...] = upper(work[:, :n])
    m_ref[...] = work[:, n:]


def head(where, mine, other):
    n = 2 * mine.shape[-1]
    vmem = pl.BlockSpec(memory_space=pltpu.VMEM)
    return pl.pallas_call(
        head_kernel,
        out_shape=(jax.ShapeDtypeStruct((n, n), jnp.float32),) * 2,
        in_specs=[pl.BlockSpec(memory_space=pltpu.SMEM), vmem, vmem],
        out_specs=(vmem, vmem),
        scratch_shapes=[pltpu.VMEM((n, 2 * n), jnp.float32)],
        compiler_params=pltpu.CompilerParams(vmem_limit_bytes=32 * 2**20),
        cost_estimate=pl.CostEstimate(flops=30 * 10**9, bytes_accessed=4 * n * n * 4, transcendentals=0),
        name="head_factor",
    )(where, mine, other)


def tail_kernel(where, r_aa, m_aa, ab_mine, ab_other, bb_mine, bb_other, out_ref, ab, bb):
    n = r_aa.shape[0]
    width = out_ref.shape[0]
    place(ab, where, ab_mine, ab_other)
    place(bb, where, bb_mine, bb_other)
    ab[...] = dot(m_aa[...], ab[...])
    bb[...] = bb[...] - tdot(ab[...], ab[...])
    eliminate(bb, n)
    bb[...] = upper(bb[...])
    r, k, right = where[0], where[1], where[2]
    rows = pl.ds(pl.multiple_of(lax.rem(r, 2) * width, width), width)
    cols = pl.ds(pl.multiple_of(k * width, width), width)
    top = r < 2

    @pl.when(jnp.logical_and(top, right == 0))
    def _():
        out_ref[...] = r_aa[rows, cols]

    @pl.when(jnp.logical_and(top, right == 1))
    def _():
        out_ref[...] = ab[rows, cols]

    @pl.when(jnp.logical_and(jnp.logical_not(top), right == 0))
    def _():
        out_ref[...] = jnp.zeros_like(out_ref)

    @pl.when(jnp.logical_and(jnp.logical_not(top), right == 1))
    def _():
        out_ref[...] = bb[rows, cols]


def tail(where, r_aa, m_aa, ab_mine, ab_other, bb_mine, bb_other):
    n = r_aa.shape[0]
    vmem = pl.BlockSpec(memory_space=pltpu.VMEM)
    return pl.pallas_call(
        tail_kernel,
        out_shape=jax.ShapeDtypeStruct((n // 2, n // 2), jnp.float32),
        in_specs=[pl.BlockSpec(memory_space=pltpu.SMEM)] + [vmem] * 6,
        out_specs=vmem,
        scratch_shapes=[pltpu.VMEM((n, n), jnp.float32)] * 2,
        compiler_params=pltpu.CompilerParams(vmem_limit_bytes=32 * 2**20),
        cost_estimate=pl.CostEstimate(flops=30 * 10**9, bytes_accessed=4 * n * n * 4, transcendentals=0),
        name="tail_factor",
    )(where, r_aa, m_aa, ab_mine, ab_other, bb_mine, bb_other)


def shards(own_rows, child_blocks, child_parent, child_live, child_first):
    front_id = lax.axis_index("front")
    row_id = lax.axis_index("row")
    col_id = lax.axis_index("col")
    side, core = col_id // 2, col_id % 2
    nfront, nrow = lax.axis_size("front"), lax.axis_size("row")
    own = own_rows[0]
    slots, child_rows, width = child_blocks.shape[1:]
    parents = lax.dynamic_slice_in_dim(child_parent, front_id, 1, 0)[0]
    live = lax.dynamic_slice_in_dim(child_live, front_id, 1, 0)[0]
    first = lax.dynamic_slice_in_dim(child_first, front_id, 1, 0)[0]
    row_index = row_id * child_rows + jnp.arange(child_rows, dtype=jnp.int32)
    col_index = col_id * width + jnp.arange(width, dtype=jnp.int32)
    keep = (row_index[None, :, None] < live[:, None, None]) & (
        col_index[None, None, :] >= PANEL * first[:, None, None]
    )
    kids = jnp.where(keep, child_blocks[0], 0.0)

    across = [(c, c ^ 2) for c in range(4)]
    beside = [(c, c ^ 1) for c in range(4)]

    def half(x, which, axis):
        size = x.shape[axis] // 2
        return lax.dynamic_slice_in_dim(x, which * size, size, axis)

    def turn(x):
        return jnp.where(side == 0, jnp.swapaxes(x, -1, -2), x)

    def ring_sum(blocks):
        n = blocks.shape[0]
        quarters = blocks.reshape(n, nrow, width // nrow, width)
        total = lax.dynamic_index_in_dim(quarters, row_id, 1, keepdims=False)
        for s in range(1, nrow):
            piece = lax.dynamic_index_in_dim(quarters, (row_id + s) % nrow, 1, keepdims=False)
            total = total + lax.ppermute(piece, "row", [(i, (i + s) % nrow) for i in range(nrow)])
        return total

    def ring_gather(piece):
        parts = [piece]
        for s in range(1, nrow):
            parts.append(lax.ppermute(piece, "row", [(i, (i + s) % nrow) for i in range(nrow)]))
        return jnp.stack(parts)

    def to_right(pair):
        same = lax.ppermute(pair[..., 0, :, :], "col", [(0, 2), (1, 3)])
        cross = lax.ppermute(pair[..., 1, :, :], "col", [(0, 3), (1, 2)])
        return pair + jnp.stack([same, cross], axis=-3)

    kid_far = lax.ppermute(half(kids, side, 1), "col", across)
    kid_near = lax.ppermute(kids, "col", beside)
    kid_mine_half = half(kids, 1 - side, 1)
    kid_near_half = half(kid_near, 1 - side, 1)

    def batch(x, y):
        return jnp.einsum("sik,sil->skl", x, y, precision=HI)

    kid_diag = jnp.stack([batch(kids, kids), batch(kids, kid_near)], axis=1)
    kid_cross = turn(jnp.stack([batch(kid_far, kid_mine_half), batch(kid_far, kid_near_half)], axis=1))

    own_send = half(own, side, 0)
    own_near = lax.ppermute(own, "col", beside)
    own_mine_half = half(own, 1 - side, 0)
    own_near_half = half(own_near, 1 - side, 0)
    far, start = [], 0
    for rows in CHUNKS:
        far.append(lax.ppermute(own_send[start : start + rows], "col", across))
        start += rows
    own_diag = jnp.stack([tdot(own, own), tdot(own, own_near)])

    kid_all = jnp.concatenate([kid_diag, kid_cross], axis=1)
    kid_sum = ring_sum(kid_all.reshape(slots * 4, width, width)).reshape(slots, 4, width // nrow, width)
    kid_sum = jnp.concatenate([kid_sum[:, :2], to_right(kid_sum[:, 2:])], axis=1)
    half_front = nfront // 2
    hi, lo = front_id // half_front, front_id % half_front
    onehot = (parents[:, None] == jnp.arange(nfront, dtype=jnp.int32)[None, :]).astype(jnp.float32)
    routed = sum(onehot[s][:, None, None, None] * kid_sum[s][None] for s in range(slots))
    routed = routed.reshape((2, half_front) + kid_sum.shape[1:])
    mine = lax.dynamic_index_in_dim(routed, lo, 1, keepdims=False)
    for s in range(1, half_front):
        piece = lax.dynamic_index_in_dim(routed, (lo + s) % half_front, 1, keepdims=False)
        perm = [(h * half_front + i, h * half_front + (i + s) % half_front) for h in range(2) for i in range(half_front)]
        mine = mine + lax.ppermute(piece, "front", perm)
    twin = [(f, (f + half_front) % nfront) for f in range(nfront)]
    for_twin = lax.dynamic_index_in_dim(mine, 1 - hi, 0, keepdims=False)
    kid_part = lax.dynamic_index_in_dim(mine, hi, 0, keepdims=False) + lax.ppermute(for_twin, "front", twin)

    where = jnp.stack([row_id, core, side]).astype(jnp.int32)
    diag = ring_sum(own_diag) + kid_part[:2]
    left = jnp.where(side == 0, diag, lax.ppermute(diag, "col", [(0, 2), (1, 3)]))
    aa = ring_gather(left)
    r_aa, m_aa = head(where, aa, lax.ppermute(aa, "col", beside))
    bb = ring_gather(diag)
    bb_other = lax.ppermute(bb, "col", beside)

    near_acc = mine_acc = 0.0
    start = 0
    for rows, got in zip(CHUNKS, far):
        mine_acc = mine_acc + tdot(got, own_mine_half[start : start + rows])
        near_acc = near_acc + tdot(got, own_near_half[start : start + rows])
        start += rows
    cross = ring_sum(turn(jnp.stack([mine_acc, near_acc])))
    cross = to_right(cross) + kid_part[2:]
    ab = ring_gather(cross)
    out = tail(where, r_aa, m_aa, ab, lax.ppermute(ab, "col", beside), bb, bb_other)
    return out[None]


def solution(mesh):
    in_specs = (P("front", "row", "col"), P("front", None, "row", "col"), P(), P(), P())
    out_specs = P("front", "row", "col")
    return jax.shard_map(shards, mesh=mesh, in_specs=in_specs, out_specs=out_specs, check_vma=False)
```

```python
import jax
import jax.numpy as jnp
from jax import lax
from jax.experimental import pallas as pl
from jax.experimental.pallas import tpu as pltpu
from jax.sharding import PartitionSpec as P

PANEL = 64
NB = 128
SUB = 8
LIGHT = pl.CostEstimate(flops=1000, bytes_accessed=1000, transcendentals=0)


def spread(x):
    return jnp.broadcast_to(x, (SUB, NB))


def column(strip, at):
    return spread(strip[:, at:at + 1])


def diag_factor(block):
    rows = lax.broadcasted_iota(jnp.int32, (SUB, NB), 0)
    lanes = lax.broadcasted_iota(jnp.int32, (SUB, NB), 1)
    count = NB // SUB
    a = [block[SUB * s:SUB * (s + 1), :] for s in range(count)]
    e = [jnp.where(lanes == rows + SUB * s, 1.0, 0.0) for s in range(count)]
    cols = [column(a[0], k) for k in range(SUB)]
    for s in range(count):
        at = SUB * s
        left, right = a[s], e[s]
        near = [t for t in (s + 1, s + 2) if t < count]
        panel = {t: [column(a[t], at + k) for k in range(SUB)] for t in near}
        ahead = [column(a[s + 1], at + SUB + k) for k in range(SUB)] if near else []
        lrows, rrows = [], []
        for k in range(SUB):
            masked = jnp.where(rows > k, cols[k], 0.0)
            rs = lax.rsqrt(spread(cols[k][k:k + 1, :]))
            m = masked * rs
            lrow = spread(left[k:k + 1, :]) * rs
            rrow = spread(right[k:k + 1, :]) * rs
            lrows.append(lrow)
            rrows.append(rrow)
            left = jnp.where(rows == k, lrow, left - m * lrow)
            right = jnp.where(rows == k, rrow, right - m * rrow)
            for t in near:
                panel[t][k] = panel[t][k] * rs
            for l in range(k + 1, SUB):
                head = spread(cols[l][k:k + 1, :]) * rs
                cols[l] = cols[l] - m * head
                for t in near:
                    panel[t][l] = panel[t][l] - panel[t][k] * head
            if near:
                own = panel[s + 1][k]
                ahead = [ahead[l] - own * spread(own[l:l + 1, :]) for l in range(SUB)]
        a[s] = jnp.where(lanes >= rows + at, left, 0.0)
        e[s] = right
        for t in near:
            for k in range(SUB):
                a[t] = a[t] - panel[t][k] * lrows[k]
                e[t] = e[t] - panel[t][k] * rrows[k]
        cols = ahead
        if s + 3 < count:
            turned = left.T
            for t in range(s + 3, count):
                for k in range(SUB):
                    mt = column(turned[SUB * t:SUB * (t + 1), :], k)
                    a[t] = a[t] - mt * lrows[k]
                    e[t] = e[t] - mt * rrows[k]
    return jnp.concatenate(a, 0), jnp.concatenate(e, 0)


def split(value):
    high = value.astype(jnp.bfloat16)
    return high, (value - high.astype(jnp.float32)).astype(jnp.bfloat16)


def mul(x, y, contract):
    d = lambda p, q: lax.dot_general(p, q, (((contract,), (0,)), ((), ())), preferred_element_type=jnp.float32)
    return d(x[0], y[0]) + (d(x[0], y[1]) + d(x[1], y[0]))


def eliminate(work, inv):
    n = work.shape[0]
    for at in range(0, n, NB):
        here, past = slice(at, at + NB), slice(at + NB, n)
        r, m = diag_factor(work[here, here])
        work[here, here] = r
        ms = split(m)
        more = at + NB < n
        if more:
            row = mul(ms, split(work[here, past]), 1)
            work[here, past] = row
            rows = split(row)
        if inv is not None:
            if at:
                inv[here, :at] = mul(ms, split(inv[here, :at]), 1)
            inv[here, here] = m
        if more:
            for t in range(at + NB, n, NB):
                lhs = tuple(x[:, t - at - NB:t - at] for x in rows)
                rhs = tuple(x[:, t - at - NB:] for x in rows)
                work[t:t + NB, t:] = work[t:t + NB, t:] - mul(lhs, rhs, 0)
            if inv is not None:
                es = split(inv[here, :at + NB])
                inv[past, :at + NB] = inv[past, :at + NB] - mul(rows, es, 0)


def upper(x):
    return jnp.where(
        lax.broadcasted_iota(jnp.int32, x.shape, 1) >= lax.broadcasted_iota(jnp.int32, x.shape, 0), x, 0.0
    )


def place(ref, ids, mine, other):
    ring, _, part, width = mine.shape
    r, k = ids[1], lax.rem(ids[2], 2)
    for source, core in ((mine, k), (other, 1 - k)):
        for s in range(ring):
            q = lax.rem(r - s + ring, ring)
            at = pl.ds(pl.multiple_of(core * width + q * part, part), part)
            ref[at, pl.ds(pl.multiple_of(core * width, width), width)] = source[s, 0]
            ref[at, pl.ds(pl.multiple_of((1 - core) * width, width), width)] = source[s, 1]


def head_kernel(ids, mine, other, after, r_ref, m_ref):
    place(r_ref, ids, mine, other)
    m_ref[...] = jnp.zeros_like(m_ref)
    eliminate(r_ref, m_ref)
    r_ref[...] = upper(r_ref[...])


def head(ids, mine, other, after):
    n = 2 * mine.shape[-1]
    vmem = pl.BlockSpec(memory_space=pltpu.VMEM)
    return pl.pallas_call(
        head_kernel,
        out_shape=(jax.ShapeDtypeStruct((n, n), jnp.float32),) * 2,
        in_specs=[pl.BlockSpec(memory_space=pltpu.SMEM), vmem, vmem, pl.BlockSpec(memory_space=pl.ANY)],
        out_specs=(vmem, vmem),
        compiler_params=pltpu.CompilerParams(vmem_limit_bytes=32 * 2**20),
        cost_estimate=pl.CostEstimate(flops=20 * 10**9, bytes_accessed=4 * n * n * 4, transcendentals=0),
        name="head_factor",
    )(ids, mine, other, after)


def tail_kernel(ids, r_aa, m_aa, ab_mine, ab_other, bb_mine, bb_other, out_ref, ab, bb):
    width = out_ref.shape[0]
    place(ab, ids, ab_mine, ab_other)
    place(bb, ids, bb_mine, bb_other)
    ab[...] = mul(split(m_aa[...]), split(ab[...]), 1)
    cross = split(ab[...])
    bb[...] = bb[...] - mul(cross, cross, 0)
    eliminate(bb, None)
    bb[...] = upper(bb[...])
    r, k, right = ids[1], lax.rem(ids[2], 2), ids[2] // 2
    rows = pl.ds(pl.multiple_of(lax.rem(r, 2) * width, width), width)
    cols = pl.ds(pl.multiple_of(k * width, width), width)
    top = r < 2

    @pl.when(jnp.logical_and(top, right == 0))
    def _():
        out_ref[...] = r_aa[rows, cols]

    @pl.when(jnp.logical_and(top, right == 1))
    def _():
        out_ref[...] = ab[rows, cols]

    @pl.when(jnp.logical_and(jnp.logical_not(top), right == 0))
    def _():
        out_ref[...] = jnp.zeros_like(out_ref)

    @pl.when(jnp.logical_and(jnp.logical_not(top), right == 1))
    def _():
        out_ref[...] = bb[rows, cols]


def tail(ids, r_aa, m_aa, ab_mine, ab_other, bb_mine, bb_other):
    n = r_aa.shape[0]
    vmem = pl.BlockSpec(memory_space=pltpu.VMEM)
    return pl.pallas_call(
        tail_kernel,
        out_shape=jax.ShapeDtypeStruct((n // 2, n // 2), jnp.float32),
        in_specs=[pl.BlockSpec(memory_space=pltpu.SMEM)] + [vmem] * 6,
        out_specs=vmem,
        scratch_shapes=[pltpu.VMEM((n, n), jnp.float32)] * 2,
        compiler_params=pltpu.CompilerParams(vmem_limit_bytes=32 * 2**20),
        cost_estimate=LIGHT,
        name="tail_factor",
    )(ids, r_aa, m_aa, ab_mine, ab_other, bb_mine, bb_other)


def sides(ids):
    return ids[2] // 2, lax.rem(ids[2], 2)


def part(x, y):
    return lax.dot_general(x, y, (((0,), (0,)), ((), ())), preferred_element_type=jnp.float32)


def add_products(out_ref, x, ys):
    xh, xl = split(x)
    for i, ref in enumerate(ys):
        yh, yl = split(ref[...])
        out_ref[0, i] += part(xh, yh) + (part(xh, yl) + part(xl, yh))


def gram_kernel(flip, ids, x_ref, y0_ref, y1_ref, start_ref, after, out_ref):
    step = pl.program_id(1)

    @pl.when(step == 0)
    def _():
        out_ref[...] = jnp.zeros_like(out_ref) if start_ref is None else start_ref[...]

    add_products(out_ref, x_ref[...], (y0_ref, y1_ref))
    if flip:

        @pl.when(jnp.logical_and(step == pl.num_programs(1) - 1, sides(ids)[0] == 0))
        def _():
            for i in range(2):
                out_ref[0, i] = out_ref[0, i].T


def kid_kernel(far, fronts, slots, ids, x_ref, y0_ref, y1_ref, after, out_ref):
    kid = pl.program_id(0)
    side, core = sides(ids)
    rows, width = x_ref.shape
    base = ids[1] * (2 * rows) + (1 - side) * rows if far else ids[1] * rows
    inside = lax.broadcasted_iota(jnp.int32, (rows, width), 0) + base < ids[3 + ids[0] * slots + kid]
    out_ref[...] = jnp.zeros_like(out_ref)
    add_products(out_ref, jnp.where(inside, x_ref[...], 0.0), (y0_ref, y1_ref))
    edge = ids[3 + (fronts + ids[0]) * slots + kid] * PANEL
    left = 2 * (1 - side) + core if far else ids[2]
    for i in range(2):
        right = 2 * side + (core if i == 0 else 1 - core)
        keep = jnp.logical_and(
            lax.broadcasted_iota(jnp.int32, (width, width), 0) + left * width >= edge,
            lax.broadcasted_iota(jnp.int32, (width, width), 1) + right * width >= edge,
        )
        out_ref[0, i] = jnp.where(keep, out_ref[0, i], 0.0)
    if far:

        @pl.when(side == 0)
        def _():
            for i in range(2):
                out_ref[0, i] = out_ref[0, i].T


def gram(ids, x, y0, y1, grid, rows, y_at, flip=False, start=None, after=None):
    width = x.shape[1]
    batch, steps = grid
    xspec = pl.BlockSpec((rows, width), lambda b, i, ids: (b * steps + i, 0))
    yspec = pl.BlockSpec((rows, width), lambda b, i, ids: (y_at(ids, b) + i, 0))
    ospec = pl.BlockSpec((1, 2, width, width), lambda b, i, ids: (b, 0, 0, 0))
    args, specs = [x, y0, y1], [xspec, yspec, yspec]
    if start is not None:
        args.append(start)
        specs.append(ospec)
    if after is not None:
        args.append(after)
        specs.append(pl.BlockSpec(memory_space=pl.ANY))

    def body(ids, x_ref, y0_ref, y1_ref, *rest):
        gram_kernel(flip, ids, x_ref, y0_ref, y1_ref, None if start is None else rest[0], None, rest[-1])

    return pl.pallas_call(
        body,
        out_shape=jax.ShapeDtypeStruct((batch, 2, width, width), jnp.float32),
        grid_spec=pltpu.PrefetchScalarGridSpec(num_scalar_prefetch=1, grid=grid, in_specs=specs, out_specs=ospec),
        compiler_params=pltpu.CompilerParams(vmem_limit_bytes=24 * 2**20),
        cost_estimate=LIGHT,
        name="own_products",
    )(ids, *args)


def kid_gram(ids, fronts, slots, x, y0, y1, far, after):
    rows, width = x.shape[0] // slots, x.shape[1]
    xspec = pl.BlockSpec((rows, width), lambda b, ids: (b, 0))
    yspec = pl.BlockSpec((rows, width), lambda b, ids: (2 * b + 1 - ids[2] // 2, 0)) if far else xspec

    def body(ids, x_ref, y0_ref, y1_ref, after_ref, out_ref):
        kid_kernel(far, fronts, slots, ids, x_ref, y0_ref, y1_ref, after_ref, out_ref)

    return pl.pallas_call(
        body,
        out_shape=jax.ShapeDtypeStruct((slots, 2, width, width), jnp.float32),
        grid_spec=pltpu.PrefetchScalarGridSpec(
            num_scalar_prefetch=1,
            grid=(slots,),
            in_specs=[xspec, yspec, yspec, pl.BlockSpec(memory_space=pl.ANY)],
            out_specs=pl.BlockSpec((1, 2, width, width), lambda b, ids: (b, 0, 0, 0)),
        ),
        compiler_params=pltpu.CompilerParams(vmem_limit_bytes=24 * 2**20),
        cost_estimate=LIGHT,
        name="child_products",
    )(ids, x, y0, y1, after)


def route_kernel(slots, fronts, ids, *refs):
    parts, outs = refs[:4], refs[-5:]
    total = (parts[0][...] + parts[1][...]) + (parts[2][...] + parts[3][...])
    blocks = 2
    half = fronts // 2
    lo = lax.rem(ids[0], half)
    base = 3 + 2 * fronts * slots + ids[0] * slots
    for s in range(half):
        for h in range(2):
            parent = h * half + lax.rem(lo + s, half)
            piece = jnp.zeros_like(total[:blocks])
            for k in range(slots):
                kid = total[k * blocks : (k + 1) * blocks]
                piece = piece + jnp.where(ids[base + k] == parent, kid, 0.0)
            outs[s][h] = piece
    if total.shape[0] > slots * blocks:
        outs[4][...] = total[slots * blocks :]
    else:
        outs[4][...] = jnp.zeros_like(outs[4])


def route(ids, slots, fronts, parts, after):
    part, width = parts[0].shape[1:]
    vmem = pl.BlockSpec(memory_space=pltpu.VMEM)
    piece = jax.ShapeDtypeStruct((2, 2, part, width), jnp.float32)
    rest = jax.ShapeDtypeStruct((2, part, width) if parts[0].shape[0] > 2 * slots else (8, 128), jnp.float32)

    def body(ids, *refs):
        route_kernel(slots, fronts, ids, *refs)

    out = pl.pallas_call(
        body,
        out_shape=(piece,) * 4 + (rest,),
        in_specs=[pl.BlockSpec(memory_space=pltpu.SMEM)] + [vmem] * 4 + [pl.BlockSpec(memory_space=pl.ANY)],
        out_specs=(vmem,) * 5,
        cost_estimate=LIGHT,
        compiler_params=pltpu.CompilerParams(vmem_limit_bytes=16 * 2**20),
        name="child_routes",
    )(ids, *parts, after)
    return out[:4], out[4]


def add_kernel(*refs):
    refs[-1][...] = (refs[0][...] + refs[1][...]) + (refs[2][...] + refs[3][...])


def add_parts(parts, after):
    vmem = pl.BlockSpec(memory_space=pltpu.VMEM)
    return pl.pallas_call(
        add_kernel,
        out_shape=jax.ShapeDtypeStruct(parts[0].shape, jnp.float32),
        in_specs=[vmem] * 4 + [pl.BlockSpec(memory_space=pl.ANY)],
        out_specs=vmem,
        cost_estimate=LIGHT,
        compiler_params=pltpu.CompilerParams(vmem_limit_bytes=16 * 2**20),
        name="ring_total",
    )(*parts, after)


def shards(own_rows, child_blocks, child_parent, child_live, child_first):
    front_id = lax.axis_index("front")
    row_id = lax.axis_index("row")
    col_id = lax.axis_index("col")
    side = col_id // 2
    nfront, nrow = lax.axis_size("front"), lax.axis_size("row")
    ids = jnp.concatenate(
        [jnp.stack([front_id, row_id, col_id]).astype(jnp.int32), child_live.reshape(-1), child_first.reshape(-1), child_parent.reshape(-1)]
    )
    own = own_rows[0]
    own_count = own.shape[0]
    slots, child_rows, width = child_blocks.shape[1:]
    across = [(c, c ^ 2) for c in range(4)]
    beside = [(c, c ^ 1) for c in range(4)]

    def ring_send(blocks):
        n = blocks.shape[0]
        quarters = blocks.reshape(n, nrow, width // nrow, width)
        parts = [lax.dynamic_index_in_dim(quarters, row_id, 1, keepdims=False)]
        for s in range(1, nrow):
            piece = lax.dynamic_index_in_dim(quarters, (row_id + s) % nrow, 1, keepdims=False)
            parts.append(lax.ppermute(piece, "row", [(i, (i + s) % nrow) for i in range(nrow)]))
        return parts

    def ring_gather(piece):
        parts = [piece]
        for s in range(1, nrow):
            parts.append(lax.ppermute(piece, "row", [(i, (i + s) % nrow) for i in range(nrow)]))
        return jnp.stack(parts)

    half_front = nfront // 2
    hi, lo = front_id // half_front, front_id % half_front
    twin = [(f, (f + half_front) % nfront) for f in range(nfront)]

    def x_ring(pieces):
        parts = [pieces[0]]
        for s in range(1, half_front):
            perm = [
                (h * half_front + i, h * half_front + (i + s) % half_front) for h in range(2) for i in range(half_front)
            ]
            parts.append(lax.ppermute(pieces[s], "front", perm))
        return parts

    def with_twin(mine):
        for_twin = lax.dynamic_index_in_dim(mine, 1 - hi, 0, keepdims=False)
        return lax.dynamic_index_in_dim(mine, hi, 0, keepdims=False) + lax.ppermute(for_twin, "front", twin)

    kids = child_blocks[0]
    kid_half = child_rows // 2
    kid_send = lax.dynamic_slice_in_dim(kids, side * kid_half, kid_half, 1).reshape(slots * kid_half, width)
    kids = kids.reshape(slots * child_rows, width)
    half = own_count // 2
    cut = half // 2
    got_kids = lax.ppermute(kid_send, "col", across)
    kid_near = lax.ppermute(kids, "col", beside)
    own_near = lax.ppermute(own, "col", beside)
    sends = [lax.dynamic_slice_in_dim(own, side * half + at, cut, 0) for at in (0, cut)]
    got = [lax.ppermute(x, "col", across) for x in sends]

    kid_diag = kid_gram(ids, nfront, slots, kids, kids, kid_near, False, sends[0])
    rows = 1024
    own_diag = gram(ids, own, own, own_near, (1, own_count // rows), rows, lambda ids, b: 0, after=kid_diag)
    both = jnp.concatenate([kid_diag.reshape(slots * 2, width, width), own_diag[0]])
    diag_pieces, own_sum = route(ids, slots, nfront, ring_send(both), ids)
    kid_cross = kid_gram(ids, nfront, slots, got_kids, kids, kid_near, True, own_diag)
    cross_parts = ring_send(kid_cross.reshape(slots * 2, width, width))
    rows = 512
    half_at, cut_at = half // rows, cut // rows
    cross = gram(
        ids, got[0], own, own_near, (1, cut_at), rows, lambda ids, b: (1 - ids[2] // 2) * half_at, after=kid_cross
    )
    diag_mine = add_parts(x_ring(diag_pieces), cross)
    cross_pieces, _ = route(ids, slots, nfront, cross_parts, diag_mine)
    cross_mine = add_parts(x_ring(cross_pieces), ids)
    diag = own_sum + with_twin(diag_mine)
    left = jnp.where(side == 0, diag, lax.ppermute(diag, "col", [(0, 2), (1, 3)]))
    kid_cross_sum = with_twin(cross_mine)
    aa = ring_gather(left)
    aa_other = lax.ppermute(aa, "col", beside)
    bb = ring_gather(diag)
    bb_other = lax.ppermute(bb, "col", beside)

    cross = gram(
        ids, got[1], own, own_near, (1, cut_at), rows,
        lambda ids, b: (1 - ids[2] // 2) * half_at + cut_at, flip=True, start=cross, after=cross_mine,
    )
    cross = sum(ring_send(cross[0])) + kid_cross_sum
    same = lax.ppermute(cross[0], "col", [(0, 2), (1, 3)])
    swap = lax.ppermute(cross[1], "col", [(0, 3), (1, 2)])
    cross = cross + jnp.stack([same, swap])
    r_aa, m_aa = head(ids, aa, aa_other, cross)
    ab = ring_gather(cross)
    out = tail(ids, r_aa, m_aa, ab, lax.ppermute(ab, "col", beside), bb, bb_other)
    return out[None]


def solution(mesh):
    in_specs = (P("front", "row", "col"), P("front", None, "row", "col"), P(), P(), P())
    out_specs = P("front", "row", "col")
    return jax.shard_map(shards, mesh=mesh, in_specs=in_specs, out_specs=out_specs, check_vma=False)
```

```python
import jax
import jax.numpy as jnp
from jax import lax
from jax.experimental import pallas as pl
from jax.experimental.pallas import tpu as pltpu
from jax.sharding import PartitionSpec as P

PANEL = 64
NB = 128
SUB = 8
LIGHT = pl.CostEstimate(flops=1000, bytes_accessed=1000, transcendentals=0)


def spread(x):
    return jnp.broadcast_to(x, (SUB, NB))


def column(strip, at):
    return spread(strip[:, at:at + 1])


def diag_factor(block, inverse=True):
    rows = lax.broadcasted_iota(jnp.int32, (SUB, NB), 0)
    lanes = lax.broadcasted_iota(jnp.int32, (SUB, NB), 1)
    count = NB // SUB
    a = [block[SUB * s:SUB * (s + 1), :] for s in range(count)]
    e = [jnp.where(lanes == rows + SUB * s, 1.0, 0.0) for s in range(count)]
    cols = [column(a[0], k) for k in range(SUB)]
    for s in range(count):
        at = SUB * s
        left, right = a[s], e[s]
        near = [t for t in (s + 1, s + 2) if t < count]
        panel = {t: [column(a[t], at + k) for k in range(SUB)] for t in near}
        ahead = [column(a[s + 1], at + SUB + k) for k in range(SUB)] if near else []
        lrows, rrows = [], []
        for k in range(SUB):
            masked = jnp.where(rows > k, cols[k], 0.0)
            rs = lax.rsqrt(spread(cols[k][k:k + 1, :]))
            m = masked * rs
            lrow = spread(left[k:k + 1, :]) * rs
            rrow = spread(right[k:k + 1, :]) * rs
            lrows.append(lrow)
            rrows.append(rrow)
            left = jnp.where(rows == k, lrow, left - m * lrow)
            if inverse:
                right = jnp.where(rows == k, rrow, right - m * rrow)
            for t in near:
                panel[t][k] = panel[t][k] * rs
            for l in range(k + 1, SUB):
                head = spread(cols[l][k:k + 1, :]) * rs
                cols[l] = cols[l] - m * head
                for t in near:
                    panel[t][l] = panel[t][l] - panel[t][k] * head
            if near:
                own = panel[s + 1][k]
                ahead = [ahead[l] - own * spread(own[l:l + 1, :]) for l in range(SUB)]
        a[s] = jnp.where(lanes >= rows + at, left, 0.0)
        e[s] = right
        for t in near:
            for k in range(SUB):
                a[t] = a[t] - panel[t][k] * lrows[k]
                if inverse:
                    e[t] = e[t] - panel[t][k] * rrows[k]
        cols = ahead
        if s + 3 < count:
            turned = left.T
            for t in range(s + 3, count):
                for k in range(SUB):
                    mt = column(turned[SUB * t:SUB * (t + 1), :], k)
                    a[t] = a[t] - mt * lrows[k]
                    if inverse:
                        e[t] = e[t] - mt * rrows[k]
    return jnp.concatenate(a, 0), jnp.concatenate(e, 0)


def split(value):
    high = value.astype(jnp.bfloat16)
    return high, (value - high.astype(jnp.float32)).astype(jnp.bfloat16)


def mul(x, y, contract):
    d = lambda p, q: lax.dot_general(p, q, (((contract,), (0,)), ((), ())), preferred_element_type=jnp.float32)
    return d(x[0], y[0]) + (d(x[0], y[1]) + d(x[1], y[0]))


def eliminate(work, inv):
    n = work.shape[0]
    for at in range(0, n, NB):
        here, past = slice(at, at + NB), slice(at + NB, n)
        more = at + NB < n
        r, m = diag_factor(work[here, here], more or inv is not None)
        work[here, here] = r
        ms = split(m)
        if more:
            row = mul(ms, split(work[here, past]), 1)
            work[here, past] = row
            rows = split(row)
        if inv is not None:
            if at:
                inv[here, :at] = mul(ms, split(inv[here, :at]), 1)
            inv[here, here] = m
        if more:
            for t in range(at + NB, n, NB):
                lhs = tuple(x[:, t - at - NB:t - at] for x in rows)
                rhs = tuple(x[:, t - at - NB:] for x in rows)
                work[t:t + NB, t:] = work[t:t + NB, t:] - mul(lhs, rhs, 0)
            if inv is not None:
                es = split(inv[here, :at + NB])
                inv[past, :at + NB] = inv[past, :at + NB] - mul(rows, es, 0)


def upper(x):
    return jnp.where(
        lax.broadcasted_iota(jnp.int32, x.shape, 1) >= lax.broadcasted_iota(jnp.int32, x.shape, 0), x, 0.0
    )


def place(ref, ids, mine, other, first=0):
    ring, _, part, width = mine.shape
    r, k = ids[0, 1], lax.rem(ids[1, 0], 2)
    for source, core in ((mine, k), (other, 1 - k)):
        for s in range(ring):
            q = lax.rem(r - s + ring, ring)
            at = pl.ds(pl.multiple_of(core * width + q * part, part), part)
            ref[at, pl.ds(pl.multiple_of(core * width, width), width)] = source[s, first]
            ref[at, pl.ds(pl.multiple_of((1 - core) * width, width), width)] = source[s, first + 1]


def head_kernel(ids, mine, other, after, r_ref, m_ref):
    place(r_ref, ids, mine, other)
    m_ref[...] = jnp.zeros_like(m_ref)
    eliminate(r_ref, m_ref)
    r_ref[...] = upper(r_ref[...])


def head(ids, mine, other, after):
    n = 2 * mine.shape[-1]
    vmem = pl.BlockSpec(memory_space=pltpu.VMEM)
    return pl.pallas_call(
        head_kernel,
        out_shape=(jax.ShapeDtypeStruct((n, n), jnp.float32),) * 2,
        in_specs=[pl.BlockSpec(memory_space=pltpu.SMEM), vmem, vmem, pl.BlockSpec(memory_space=pl.ANY)],
        out_specs=(vmem, vmem),
        compiler_params=pltpu.CompilerParams(vmem_limit_bytes=16 * 2**20),
        cost_estimate=pl.CostEstimate(flops=20 * 10**9, bytes_accessed=4 * n * n * 4, transcendentals=0),
        name="head_factor",
    )(ids, mine, other, after)


def tail_kernel(ids, r_aa, m_aa, mine, other, out_ref, ab, bb):
    width = out_ref.shape[0]
    place(ab, ids, mine, other)
    place(bb, ids, mine, other, 2)
    ab[...] = mul(split(m_aa[...]), split(ab[...]), 1)
    cross = split(ab[...])
    bb[...] = bb[...] - mul(cross, cross, 0)
    eliminate(bb, None)
    bb[...] = upper(bb[...])
    r, k, right = ids[0, 1], lax.rem(ids[1, 0], 2), ids[1, 0] // 2
    rows = pl.ds(pl.multiple_of(lax.rem(r, 2) * width, width), width)
    cols = pl.ds(pl.multiple_of(k * width, width), width)
    top = r < 2

    @pl.when(jnp.logical_and(top, right == 0))
    def _():
        out_ref[...] = r_aa[rows, cols]

    @pl.when(jnp.logical_and(top, right == 1))
    def _():
        out_ref[...] = ab[rows, cols]

    @pl.when(jnp.logical_and(jnp.logical_not(top), right == 0))
    def _():
        out_ref[...] = jnp.zeros_like(out_ref)

    @pl.when(jnp.logical_and(jnp.logical_not(top), right == 1))
    def _():
        out_ref[...] = bb[rows, cols]


def tail(ids, r_aa, m_aa, mine, other):
    n = r_aa.shape[0]
    vmem = pl.BlockSpec(memory_space=pltpu.VMEM)
    return pl.pallas_call(
        tail_kernel,
        out_shape=jax.ShapeDtypeStruct((n // 2, n // 2), jnp.float32),
        in_specs=[pl.BlockSpec(memory_space=pltpu.SMEM)] + [vmem] * 4,
        out_specs=vmem,
        scratch_shapes=[pltpu.VMEM((n, n), jnp.float32)] * 2,
        compiler_params=pltpu.CompilerParams(vmem_limit_bytes=16 * 2**20),
        cost_estimate=LIGHT,
        name="tail_factor",
    )(ids, r_aa, m_aa, mine, other)


def sides(ids):
    return ids[1, 0] // 2, lax.rem(ids[1, 0], 2)


def part(x, y):
    return lax.dot_general(x, y, (((0,), (0,)), ((), ())), preferred_element_type=jnp.float32)


def add_products(out_ref, x, ys):
    xh, xl = split(x)
    for i, ref in enumerate(ys):
        yh, yl = split(ref[...])
        out_ref[0, i] += part(xh, yh) + (part(xh, yl) + part(xl, yh))


def gram_kernel(flip, ids, x_ref, y0_ref, y1_ref, start_ref, after, out_ref):
    step = pl.program_id(1)

    @pl.when(step == 0)
    def _():
        out_ref[...] = jnp.zeros_like(out_ref) if start_ref is None else start_ref[...]

    add_products(out_ref, x_ref[...], (y0_ref, y1_ref))
    if flip:

        @pl.when(jnp.logical_and(step == pl.num_programs(1) - 1, sides(ids)[0] == 0))
        def _():
            for i in range(2):
                out_ref[0, i] = out_ref[0, i].T


def kid_kernel(far, fronts, slots, ids, x_ref, y0_ref, y1_ref, after, out_ref):
    kid = pl.program_id(0)
    side, core = sides(ids)
    rows, width = x_ref.shape
    base = ids[0, 1] * (2 * rows) + (1 - side) * rows if far else ids[0, 1] * rows
    inside = lax.broadcasted_iota(jnp.int32, (rows, width), 0) + base < ids[2 + ids[0, 0], kid]
    out_ref[...] = jnp.zeros_like(out_ref)
    add_products(out_ref, jnp.where(inside, x_ref[...], 0.0), (y0_ref, y1_ref))
    edge = ids[2 + fronts + ids[0, 0], kid] * PANEL
    left = 2 * (1 - side) + core if far else ids[1, 0]
    for i in range(2):
        right = 2 * side + (core if i == 0 else 1 - core)
        keep = jnp.logical_and(
            lax.broadcasted_iota(jnp.int32, (width, width), 0) + left * width >= edge,
            lax.broadcasted_iota(jnp.int32, (width, width), 1) + right * width >= edge,
        )
        out_ref[0, i] = jnp.where(keep, out_ref[0, i], 0.0)
    if far:

        @pl.when(side == 0)
        def _():
            for i in range(2):
                out_ref[0, i] = out_ref[0, i].T


def gram(ids, x, y0, y1, grid, rows, y_at, flip=False, start=None, after=None, x_at=0):
    width = x.shape[1]
    batch, steps = grid
    xspec = pl.BlockSpec((rows, width), lambda b, i, ids: (x_at + b * steps + i, 0))
    yspec = pl.BlockSpec((rows, width), lambda b, i, ids: (y_at(ids, b) + i, 0))
    ospec = pl.BlockSpec((1, 2, width, width), lambda b, i, ids: (b, 0, 0, 0))
    args, specs = [x, y0, y1], [xspec, yspec, yspec]
    if start is not None:
        args.append(start)
        specs.append(ospec)
    if after is not None:
        args.append(after)
        specs.append(pl.BlockSpec(memory_space=pl.ANY))

    def body(ids, x_ref, y0_ref, y1_ref, *rest):
        gram_kernel(flip, ids, x_ref, y0_ref, y1_ref, None if start is None else rest[0], None, rest[-1])

    return pl.pallas_call(
        body,
        out_shape=jax.ShapeDtypeStruct((batch, 2, width, width), jnp.float32),
        grid_spec=pltpu.PrefetchScalarGridSpec(num_scalar_prefetch=1, grid=grid, in_specs=specs, out_specs=ospec),
        compiler_params=pltpu.CompilerParams(vmem_limit_bytes=16 * 2**20),
        cost_estimate=LIGHT,
        name="own_products",
    )(ids, *args)


def kid_gram(ids, fronts, slots, x, y0, y1, far, after):
    rows, width = y0.shape[0] // slots // (2 if far else 1), x.shape[1]
    xspec = pl.BlockSpec((rows, width), lambda b, ids: (b, 0))
    yspec = pl.BlockSpec((rows, width), lambda b, ids: (2 * b + 1 - ids[1, 0] // 2, 0)) if far else xspec

    def body(ids, x_ref, y0_ref, y1_ref, after_ref, out_ref):
        kid_kernel(far, fronts, slots, ids, x_ref, y0_ref, y1_ref, after_ref, out_ref)

    return pl.pallas_call(
        body,
        out_shape=jax.ShapeDtypeStruct((slots, 2, width, width), jnp.float32),
        grid_spec=pltpu.PrefetchScalarGridSpec(
            num_scalar_prefetch=1,
            grid=(slots,),
            in_specs=[xspec, yspec, yspec, pl.BlockSpec(memory_space=pl.ANY)],
            out_specs=pl.BlockSpec((1, 2, width, width), lambda b, ids: (b, 0, 0, 0)),
        ),
        compiler_params=pltpu.CompilerParams(vmem_limit_bytes=12 * 2**20),
        cost_estimate=LIGHT,
        name="child_products",
    )(ids, x, y0, y1, after)


def route_kernel(slots, fronts, ids, *refs):
    parts, outs = refs[:4], refs[-5:]
    total = (parts[0][...] + parts[1][...]) + (parts[2][...] + parts[3][...])
    blocks = 2
    half = fronts // 2
    lo = lax.rem(ids[0, 0], half)
    base = 2 + 2 * fronts + ids[0, 0]
    for s in range(half):
        for h in range(2):
            parent = h * half + lax.rem(lo + s, half)
            piece = jnp.zeros_like(total[:blocks])
            for k in range(slots):
                kid = total[k * blocks : (k + 1) * blocks]
                piece = piece + jnp.where(ids[base, k] == parent, kid, 0.0)
            outs[s][h] = piece
    if total.shape[0] > slots * blocks:
        outs[4][...] = total[slots * blocks :]
    else:
        outs[4][...] = jnp.zeros_like(outs[4])


def route(ids, slots, fronts, parts, after):
    part, width = parts[0].shape[1:]
    vmem = pl.BlockSpec(memory_space=pltpu.VMEM)
    piece = jax.ShapeDtypeStruct((2, 2, part, width), jnp.float32)
    rest = jax.ShapeDtypeStruct((2, part, width) if parts[0].shape[0] > 2 * slots else (8, 128), jnp.float32)

    def body(ids, *refs):
        route_kernel(slots, fronts, ids, *refs)

    out = pl.pallas_call(
        body,
        out_shape=(piece,) * 4 + (rest,),
        in_specs=[pl.BlockSpec(memory_space=pltpu.SMEM)] + [vmem] * 4 + [pl.BlockSpec(memory_space=pl.ANY)],
        out_specs=(vmem,) * 5,
        cost_estimate=LIGHT,
        compiler_params=pltpu.CompilerParams(vmem_limit_bytes=8 * 2**20),
        name="child_routes",
    )(ids, *parts, after)
    return out[:4], out[4]


def add_kernel(*refs):
    refs[-1][...] = (refs[0][...] + refs[1][...]) + (refs[2][...] + refs[3][...])


def add_parts(parts, after):
    vmem = pl.BlockSpec(memory_space=pltpu.VMEM)
    return pl.pallas_call(
        add_kernel,
        out_shape=jax.ShapeDtypeStruct(parts[0].shape, jnp.float32),
        in_specs=[vmem] * 4 + [pl.BlockSpec(memory_space=pl.ANY)],
        out_specs=vmem,
        cost_estimate=LIGHT,
        compiler_params=pltpu.CompilerParams(vmem_limit_bytes=6 * 2**20),
        name="ring_total",
    )(*parts, after)


def joined(parts, after):
    vmem = pl.BlockSpec(memory_space=pltpu.VMEM)

    def body(*refs):
        for i, ref in enumerate(refs[: len(parts)]):
            refs[-1][i] = ref[...]

    return pl.pallas_call(
        body,
        out_shape=jax.ShapeDtypeStruct((len(parts),) + parts[0].shape, jnp.float32),
        in_specs=[vmem] * len(parts) + [pl.BlockSpec(memory_space=pl.ANY)],
        out_specs=vmem,
        cost_estimate=LIGHT,
        compiler_params=pltpu.CompilerParams(vmem_limit_bytes=6 * 2**20),
        name="ring_parts",
    )(*parts, after)


def diag_total(ids, half_front, own_sum, mine, other, after):
    vmem = pl.BlockSpec(memory_space=pltpu.VMEM)

    def body(ids, own_ref, mine_ref, other_ref, after_ref, out_ref):
        out_ref[...] = own_ref[...] + mine_ref[ids[0, 0] // half_front] + other_ref[...]

    return pl.pallas_call(
        body,
        out_shape=jax.ShapeDtypeStruct(own_sum.shape, jnp.float32),
        in_specs=[pl.BlockSpec(memory_space=pltpu.SMEM)] + [vmem] * 3 + [pl.BlockSpec(memory_space=pl.ANY)],
        out_specs=vmem,
        cost_estimate=LIGHT,
        compiler_params=pltpu.CompilerParams(vmem_limit_bytes=6 * 2**20),
        name="diag_total",
    )(ids, own_sum, mine, other, after)


def far_rows(ids, kids, own, after, at, size):
    count, width = own.shape
    slots = 0 if kids is None else kids.shape[0]
    ahead = 0 if kids is None else kids.shape[1] // 2
    hbm = pl.BlockSpec(memory_space=pl.ANY)
    args = [own] + [x for x in (kids, after) if x is not None]

    def body(ids, *refs):
        out_ref, sems = refs[-2:]
        side = ids[1, 0] // 2
        start = pl.multiple_of(side * (count // 2) + at, 256)
        copies = [
            pltpu.make_async_copy(
                refs[0].at[pl.ds(start, size)], out_ref.at[pl.ds(slots * ahead, size)], sems.at[slots]
            )
        ]
        for k in range(slots):
            first = pl.multiple_of(side * ahead, ahead)
            copies.append(
                pltpu.make_async_copy(
                    refs[1].at[k, pl.ds(first, ahead)], out_ref.at[pl.ds(k * ahead, ahead)], sems.at[k]
                )
            )
        for copy in copies:
            copy.start()
        for copy in copies:
            copy.wait()

    return pl.pallas_call(
        body,
        out_shape=jax.ShapeDtypeStruct((slots * ahead + size, width), jnp.float32),
        in_specs=[pl.BlockSpec(memory_space=pltpu.SMEM)] + [hbm] * len(args),
        out_specs=pl.BlockSpec(memory_space=pltpu.VMEM),
        scratch_shapes=[pltpu.SemaphoreType.DMA((slots + 1,))],
        compiler_params=pltpu.CompilerParams(vmem_limit_bytes=6 * 2**20),
        cost_estimate=LIGHT,
        name="far_rows",
    )(ids, *args)


def shards(own_rows, child_blocks, child_parent, child_live, child_first):
    front_id = lax.axis_index("front")
    row_id = lax.axis_index("row")
    col_id = lax.axis_index("col")
    side = col_id // 2
    nfront, nrow = lax.axis_size("front"), lax.axis_size("row")
    here = jnp.stack([front_id, row_id, col_id, col_id]).astype(jnp.int32).reshape(2, 2)
    ids = jnp.concatenate([here, child_live, child_first, child_parent], axis=0)
    own = own_rows[0]
    own_count = own.shape[0]
    slots, child_rows, width = child_blocks.shape[1:]
    across = [(c, c ^ 2) for c in range(4)]
    beside = [(c, c ^ 1) for c in range(4)]

    def ring_send(blocks):
        n = blocks.shape[0]
        quarters = blocks.reshape(n, nrow, width // nrow, width)
        parts = [lax.dynamic_index_in_dim(quarters, row_id, 1, keepdims=False)]
        for s in range(1, nrow):
            piece = lax.dynamic_index_in_dim(quarters, (row_id + s) % nrow, 1, keepdims=False)
            parts.append(lax.ppermute(piece, "row", [(i, (i + s) % nrow) for i in range(nrow)]))
        return parts

    def ring_gather(piece):
        parts = [piece]
        for s in range(1, nrow):
            parts.append(lax.ppermute(piece, "row", [(i, (i + s) % nrow) for i in range(nrow)]))
        return parts

    half_front = nfront // 2
    hi, lo = front_id // half_front, front_id % half_front
    twin = [(f, (f + half_front) % nfront) for f in range(nfront)]

    def x_ring(pieces):
        parts = [pieces[0]]
        for s in range(1, half_front):
            perm = [
                (h * half_front + i, h * half_front + (i + s) % half_front) for h in range(2) for i in range(half_front)
            ]
            parts.append(lax.ppermute(pieces[s], "front", perm))
        return parts

    def from_twin(mine):
        return lax.ppermute(lax.dynamic_index_in_dim(mine, 1 - hi, 0, keepdims=False), "front", twin)

    kids = child_blocks[0].reshape(slots * child_rows, width)
    kid_half = slots * child_rows // 2
    half = own_count // 2
    cut = half // 2
    kid_near = lax.ppermute(kids, "col", beside)
    own_near = lax.ppermute(own, "col", beside)
    send = far_rows(here, child_blocks[0], own, None, 0, cut)
    got = [lax.ppermute(send, "col", across)]

    kid_diag = kid_gram(ids, nfront, slots, kids, kids, kid_near, False, send)
    got.append(lax.ppermute(far_rows(here, None, own, kid_diag, cut, half - cut), "col", across))
    rows = 1024
    own_diag = gram(ids, own, own, own_near, (1, own_count // rows), rows, lambda ids, b: 0, after=kid_diag)
    both = jnp.concatenate([kid_diag.reshape(slots * 2, width, width), own_diag[0]])
    diag_pieces, own_sum = route(ids, slots, nfront, ring_send(both), ids)
    kid_cross = kid_gram(ids, nfront, slots, got[0], kids, kid_near, True, own_diag)
    cross_parts = ring_send(kid_cross.reshape(slots * 2, width, width))
    rows = 512
    half_at, cut_at = half // rows, cut // rows
    cross = gram(
        ids, got[0], own, own_near, (1, cut_at), rows, lambda ids, b: (1 - ids[1, 0] // 2) * half_at,
        after=kid_cross, x_at=kid_half // rows,
    )
    diag_mine = add_parts(x_ring(diag_pieces), cross)
    cross_pieces, _ = route(ids, slots, nfront, cross_parts, diag_mine)
    cross = gram(
        ids, got[1], own, own_near, (1, cut_at), rows,
        lambda ids, b: (1 - ids[1, 0] // 2) * half_at + cut_at, flip=True, start=cross, after=diag_mine,
    )
    diag = diag_total(ids, half_front, own_sum, diag_mine, from_twin(diag_mine), cross)
    left = jnp.where(side == 0, diag, lax.ppermute(diag, "col", [(0, 2), (1, 3)]))
    cross = add_parts(ring_send(cross[0]), left)
    cross_mine = add_parts(x_ring(cross_pieces), cross)
    kid_cross_sum = lax.dynamic_index_in_dim(cross_mine, hi, 0, keepdims=False) + from_twin(cross_mine)
    aa = jnp.stack(ring_gather(left))
    aa_other = lax.ppermute(aa, "col", beside)

    cross = cross + kid_cross_sum
    same = lax.ppermute(cross[0], "col", [(0, 2), (1, 3)])
    swap = lax.ppermute(cross[1], "col", [(0, 3), (1, 2)])
    right = jnp.concatenate([cross + jnp.stack([same, swap]), diag])
    r_aa, m_aa = head(ids, aa, aa_other, right)
    right = joined(ring_gather(right), m_aa)
    out = tail(ids, r_aa, m_aa, right, lax.ppermute(right, "col", beside))
    return out[None]


def solution(mesh):
    in_specs = (P("front", "row", "col"), P("front", None, "row", "col"), P(), P(), P())
    out_specs = P("front", "row", "col")
    return jax.shard_map(shards, mesh=mesh, in_specs=in_specs, out_specs=out_specs, check_vma=False)
```

```python
import jax
import jax.numpy as jnp
from jax import lax
from jax.experimental import pallas as pl
from jax.experimental.pallas import tpu as pltpu
from jax.sharding import PartitionSpec as P

PANEL = 64
NB = 128
SUB = 8
LIGHT = pl.CostEstimate(flops=1000, bytes_accessed=1000, transcendentals=0)


def spread(x):
    return jnp.broadcast_to(x, (SUB, NB))


def column(strip, at):
    return spread(strip[:, at:at + 1])


def diag_factor(block):
    rows = lax.broadcasted_iota(jnp.int32, (SUB, NB), 0)
    lanes = lax.broadcasted_iota(jnp.int32, (SUB, NB), 1)
    count = NB // SUB
    both = [block[SUB * s:SUB * (s + 1), :] for s in range(count)]
    factor, inverse = [], []
    def read(t, at):
        return [column(both[t], at + k) for k in range(SUB)] if t < count else []

    cols, first, second = read(0, 0), read(1, 0), read(2, 0)
    for s in range(count):
        at = SUB * s
        left = both[s]
        right = jnp.where(lanes < at, left, jnp.where(lanes == rows + at, 1.0, 0.0))
        ahead, ahead_first = read(s + 1, at + SUB), read(s + 2, at + SUB)
        done = lanes < at + SUB
        band = jnp.logical_and(lanes >= at, done)
        sources = []
        for k in range(SUB):
            masked = jnp.where(rows > k, cols[k], 0.0)
            rs = lax.rsqrt(spread(cols[k][k:k + 1, :]))
            m = masked * rs
            lrow = spread(left[k:k + 1, :]) * rs
            rrow = spread(right[k:k + 1, :]) * rs
            sources.append(jnp.where(done, rrow, lrow))
            left = jnp.where(rows == k, lrow, left - m * lrow)
            right = jnp.where(rows == k, rrow, right - m * rrow)
            for panel in (first, second):
                if panel:
                    panel[k] = panel[k] * rs
            for l in range(k + 1, SUB):
                head = spread(cols[l][k:k + 1, :]) * rs
                cols[l] = cols[l] - m * head
                for panel in (first, second):
                    if panel:
                        panel[l] = panel[l] - panel[k] * head
            if first:
                for l in range(SUB):
                    scale = spread(first[k][l:l + 1, :])
                    ahead[l] = ahead[l] - first[k] * scale
                    if second:
                        ahead_first[l] = ahead_first[l] - second[k] * scale
        factor.append(jnp.where(lanes >= rows + at, left, 0.0))
        inverse.append(right)
        for t, panel in ((s + 1, first), (s + 2, second)):
            if panel:
                both[t] = jnp.where(band, 0.0, both[t])
                for k in range(SUB):
                    both[t] = both[t] - panel[k] * sources[k]
        if s + 3 < count:
            source = split(jnp.where(done, right, left))
            update = mul(split(factor[s]), source, 0)
            for t in range(s + 3, count):
                both[t] = jnp.where(band, 0.0, both[t]) - update[SUB * t:SUB * (t + 1), :]
        cols, first, second = ahead, ahead_first, read(s + 3, at + SUB)
    return jnp.concatenate(factor, 0), jnp.concatenate(inverse, 0)


def split(value):
    high = value.astype(jnp.bfloat16)
    return high, (value - high.astype(jnp.float32)).astype(jnp.bfloat16)


def mul(x, y, contract):
    d = lambda p, q: lax.dot_general(p, q, (((contract,), (0,)), ((), ())), preferred_element_type=jnp.float32)
    return d(x[0], y[0]) + (d(x[0], y[1]) + d(x[1], y[0]))


def eliminate(work, inv):
    n = work.shape[0]
    for at in range(0, n, NB):
        here, past = slice(at, at + NB), slice(at + NB, n)
        r, m = diag_factor(work[here, here])
        work[here, here] = r
        ms = split(m)
        more = at + NB < n
        if more:
            row = mul(ms, split(work[here, past]), 1)
            work[here, past] = row
            rows = split(row)
        if inv is not None:
            if at:
                inv[here, :at] = mul(ms, split(inv[here, :at]), 1)
            inv[here, here] = m
        if more:
            for t in range(at + NB, n, NB):
                lhs = tuple(x[:, t - at - NB:t - at] for x in rows)
                rhs = tuple(x[:, t - at - NB:] for x in rows)
                work[t:t + NB, t:] = work[t:t + NB, t:] - mul(lhs, rhs, 0)
            if inv is not None:
                es = split(inv[here, :at + NB])
                inv[past, :at + NB] = inv[past, :at + NB] - mul(rows, es, 0)


def upper(x):
    return jnp.where(
        lax.broadcasted_iota(jnp.int32, x.shape, 1) >= lax.broadcasted_iota(jnp.int32, x.shape, 0), x, 0.0
    )


def place(ref, ids, mine, other, first=0):
    ring, _, part, width = mine.shape
    r, k = ids[0, 1], lax.rem(ids[1, 0], 2)
    for source, core in ((mine, k), (other, 1 - k)):
        for s in range(ring):
            q = lax.rem(r - s + ring, ring)
            at = pl.ds(pl.multiple_of(core * width + q * part, part), part)
            ref[at, pl.ds(pl.multiple_of(core * width, width), width)] = source[s, first]
            ref[at, pl.ds(pl.multiple_of((1 - core) * width, width), width)] = source[s, first + 1]


def head_kernel(ids, mine, other, after, r_ref, m_ref):
    place(r_ref, ids, mine, other)
    m_ref[...] = jnp.zeros_like(m_ref)
    eliminate(r_ref, m_ref)
    r_ref[...] = upper(r_ref[...])


def head(ids, mine, other, after):
    n = 2 * mine.shape[-1]
    vmem = pl.BlockSpec(memory_space=pltpu.VMEM)
    return pl.pallas_call(
        head_kernel,
        out_shape=(jax.ShapeDtypeStruct((n, n), jnp.float32),) * 2,
        in_specs=[pl.BlockSpec(memory_space=pltpu.SMEM), vmem, vmem, pl.BlockSpec(memory_space=pl.ANY)],
        out_specs=(vmem, vmem),
        compiler_params=pltpu.CompilerParams(vmem_limit_bytes=16 * 2**20),
        cost_estimate=pl.CostEstimate(flops=20 * 10**9, bytes_accessed=4 * n * n * 4, transcendentals=0),
        name="head_factor",
    )(ids, mine, other, after)


def tail_kernel(ids, r_aa, m_aa, mine, other, out_ref, ab, bb):
    width = out_ref.shape[0]
    place(ab, ids, mine, other)
    place(bb, ids, mine, other, 2)
    ab[...] = mul(split(m_aa[...]), split(ab[...]), 1)
    cross = split(ab[...])
    bb[...] = bb[...] - mul(cross, cross, 0)
    eliminate(bb, None)
    bb[...] = upper(bb[...])
    r, k, right = ids[0, 1], lax.rem(ids[1, 0], 2), ids[1, 0] // 2
    rows = pl.ds(pl.multiple_of(lax.rem(r, 2) * width, width), width)
    cols = pl.ds(pl.multiple_of(k * width, width), width)
    top = r < 2

    @pl.when(jnp.logical_and(top, right == 0))
    def _():
        out_ref[...] = r_aa[rows, cols]

    @pl.when(jnp.logical_and(top, right == 1))
    def _():
        out_ref[...] = ab[rows, cols]

    @pl.when(jnp.logical_and(jnp.logical_not(top), right == 0))
    def _():
        out_ref[...] = jnp.zeros_like(out_ref)

    @pl.when(jnp.logical_and(jnp.logical_not(top), right == 1))
    def _():
        out_ref[...] = bb[rows, cols]


def tail(ids, r_aa, m_aa, mine, other):
    n = r_aa.shape[0]
    vmem = pl.BlockSpec(memory_space=pltpu.VMEM)
    return pl.pallas_call(
        tail_kernel,
        out_shape=jax.ShapeDtypeStruct((n // 2, n // 2), jnp.float32),
        in_specs=[pl.BlockSpec(memory_space=pltpu.SMEM)] + [vmem] * 4,
        out_specs=vmem,
        scratch_shapes=[pltpu.VMEM((n, n), jnp.float32)] * 2,
        compiler_params=pltpu.CompilerParams(vmem_limit_bytes=16 * 2**20),
        cost_estimate=LIGHT,
        name="tail_factor",
    )(ids, r_aa, m_aa, mine, other)


def sides(ids):
    return ids[1, 0] // 2, lax.rem(ids[1, 0], 2)


def part(x, y):
    return lax.dot_general(x, y, (((0,), (0,)), ((), ())), preferred_element_type=jnp.float32)


def add_products(out_ref, x, ys):
    xh, xl = split(x)
    for i, ref in enumerate(ys):
        yh, yl = split(ref[...])
        out_ref[0, i] += part(xh, yh) + (part(xh, yl) + part(xl, yh))


def gram_kernel(flip, ids, x_ref, y0_ref, y1_ref, start_ref, after, out_ref):
    step = pl.program_id(1)

    @pl.when(step == 0)
    def _():
        out_ref[...] = jnp.zeros_like(out_ref) if start_ref is None else start_ref[...]

    add_products(out_ref, x_ref[...], (y0_ref, y1_ref))
    if flip:

        @pl.when(jnp.logical_and(step == pl.num_programs(1) - 1, sides(ids)[0] == 0))
        def _():
            for i in range(2):
                out_ref[0, i] = out_ref[0, i].T


def kid_kernel(far, fronts, slots, ids, x_ref, y0_ref, y1_ref, after, out_ref):
    kid = pl.program_id(0)
    side, core = sides(ids)
    rows, width = x_ref.shape
    base = ids[0, 1] * (2 * rows) + (1 - side) * rows if far else ids[0, 1] * rows
    inside = lax.broadcasted_iota(jnp.int32, (rows, width), 0) + base < ids[2 + ids[0, 0], kid]
    out_ref[...] = jnp.zeros_like(out_ref)
    add_products(out_ref, jnp.where(inside, x_ref[...], 0.0), (y0_ref, y1_ref))
    edge = ids[2 + fronts + ids[0, 0], kid] * PANEL
    left = 2 * (1 - side) + core if far else ids[1, 0]
    for i in range(2):
        right = 2 * side + (core if i == 0 else 1 - core)
        keep = jnp.logical_and(
            lax.broadcasted_iota(jnp.int32, (width, width), 0) + left * width >= edge,
            lax.broadcasted_iota(jnp.int32, (width, width), 1) + right * width >= edge,
        )
        out_ref[0, i] = jnp.where(keep, out_ref[0, i], 0.0)
    if far:

        @pl.when(side == 0)
        def _():
            for i in range(2):
                out_ref[0, i] = out_ref[0, i].T


def gram(ids, x, y0, y1, grid, rows, y_at, flip=False, start=None, after=None, x_at=0):
    width = x.shape[1]
    batch, steps = grid
    xspec = pl.BlockSpec((rows, width), lambda b, i, ids: (x_at + b * steps + i, 0))
    yspec = pl.BlockSpec((rows, width), lambda b, i, ids: (y_at(ids, b) + i, 0))
    ospec = pl.BlockSpec((1, 2, width, width), lambda b, i, ids: (b, 0, 0, 0))
    args, specs = [x, y0, y1], [xspec, yspec, yspec]
    if start is not None:
        args.append(start)
        specs.append(ospec)
    if after is not None:
        args.append(after)
        specs.append(pl.BlockSpec(memory_space=pl.ANY))

    def body(ids, x_ref, y0_ref, y1_ref, *rest):
        gram_kernel(flip, ids, x_ref, y0_ref, y1_ref, None if start is None else rest[0], None, rest[-1])

    return pl.pallas_call(
        body,
        out_shape=jax.ShapeDtypeStruct((batch, 2, width, width), jnp.float32),
        grid_spec=pltpu.PrefetchScalarGridSpec(num_scalar_prefetch=1, grid=grid, in_specs=specs, out_specs=ospec),
        compiler_params=pltpu.CompilerParams(vmem_limit_bytes=16 * 2**20),
        cost_estimate=LIGHT,
        name="own_products",
    )(ids, *args)


def kid_gram(ids, fronts, slots, x, y0, y1, far, after):
    rows, width = y0.shape[0] // slots // (2 if far else 1), x.shape[1]
    xspec = pl.BlockSpec((rows, width), lambda b, ids: (b, 0))
    yspec = pl.BlockSpec((rows, width), lambda b, ids: (2 * b + 1 - ids[1, 0] // 2, 0)) if far else xspec

    def body(ids, x_ref, y0_ref, y1_ref, after_ref, out_ref):
        kid_kernel(far, fronts, slots, ids, x_ref, y0_ref, y1_ref, after_ref, out_ref)

    return pl.pallas_call(
        body,
        out_shape=jax.ShapeDtypeStruct((slots, 2, width, width), jnp.float32),
        grid_spec=pltpu.PrefetchScalarGridSpec(
            num_scalar_prefetch=1,
            grid=(slots,),
            in_specs=[xspec, yspec, yspec, pl.BlockSpec(memory_space=pl.ANY)],
            out_specs=pl.BlockSpec((1, 2, width, width), lambda b, ids: (b, 0, 0, 0)),
        ),
        compiler_params=pltpu.CompilerParams(vmem_limit_bytes=12 * 2**20),
        cost_estimate=LIGHT,
        name="child_products",
    )(ids, x, y0, y1, after)


def route_kernel(slots, fronts, ids, *refs):
    parts, outs = refs[:4], refs[-5:]
    total = (parts[0][...] + parts[1][...]) + (parts[2][...] + parts[3][...])
    blocks = 2
    half = fronts // 2
    lo = lax.rem(ids[0, 0], half)
    base = 2 + 2 * fronts + ids[0, 0]
    for s in range(half):
        for h in range(2):
            parent = h * half + lax.rem(lo + s, half)
            piece = jnp.zeros_like(total[:blocks])
            for k in range(slots):
                kid = total[k * blocks : (k + 1) * blocks]
                piece = piece + jnp.where(ids[base, k] == parent, kid, 0.0)
            outs[s][h] = piece
    if total.shape[0] > slots * blocks:
        outs[4][...] = total[slots * blocks :]
    else:
        outs[4][...] = jnp.zeros_like(outs[4])


def route(ids, slots, fronts, parts, after):
    part, width = parts[0].shape[1:]
    vmem = pl.BlockSpec(memory_space=pltpu.VMEM)
    piece = jax.ShapeDtypeStruct((2, 2, part, width), jnp.float32)
    rest = jax.ShapeDtypeStruct((2, part, width) if parts[0].shape[0] > 2 * slots else (8, 128), jnp.float32)

    def body(ids, *refs):
        route_kernel(slots, fronts, ids, *refs)

    out = pl.pallas_call(
        body,
        out_shape=(piece,) * 4 + (rest,),
        in_specs=[pl.BlockSpec(memory_space=pltpu.SMEM)] + [vmem] * 4 + [pl.BlockSpec(memory_space=pl.ANY)],
        out_specs=(vmem,) * 5,
        cost_estimate=LIGHT,
        compiler_params=pltpu.CompilerParams(vmem_limit_bytes=8 * 2**20),
        name="child_routes",
    )(ids, *parts, after)
    return out[:4], out[4]


def add_kernel(*refs):
    refs[-1][...] = (refs[0][...] + refs[1][...]) + (refs[2][...] + refs[3][...])


def add_parts(parts, after):
    vmem = pl.BlockSpec(memory_space=pltpu.VMEM)
    return pl.pallas_call(
        add_kernel,
        out_shape=jax.ShapeDtypeStruct(parts[0].shape, jnp.float32),
        in_specs=[vmem] * 4 + [pl.BlockSpec(memory_space=pl.ANY)],
        out_specs=vmem,
        cost_estimate=LIGHT,
        compiler_params=pltpu.CompilerParams(vmem_limit_bytes=6 * 2**20),
        name="ring_total",
    )(*parts, after)


def joined(parts, after):
    vmem = pl.BlockSpec(memory_space=pltpu.VMEM)

    def body(*refs):
        for i, ref in enumerate(refs[: len(parts)]):
            refs[-1][i] = ref[...]

    return pl.pallas_call(
        body,
        out_shape=jax.ShapeDtypeStruct((len(parts),) + parts[0].shape, jnp.float32),
        in_specs=[vmem] * len(parts) + [pl.BlockSpec(memory_space=pl.ANY)],
        out_specs=vmem,
        cost_estimate=LIGHT,
        compiler_params=pltpu.CompilerParams(vmem_limit_bytes=6 * 2**20),
        name="ring_parts",
    )(*parts, after)


def diag_total(ids, half_front, own_sum, mine, other, after):
    vmem = pl.BlockSpec(memory_space=pltpu.VMEM)

    def body(ids, own_ref, mine_ref, other_ref, after_ref, out_ref):
        out_ref[...] = own_ref[...] + mine_ref[ids[0, 0] // half_front] + other_ref[...]

    return pl.pallas_call(
        body,
        out_shape=jax.ShapeDtypeStruct(own_sum.shape, jnp.float32),
        in_specs=[pl.BlockSpec(memory_space=pltpu.SMEM)] + [vmem] * 3 + [pl.BlockSpec(memory_space=pl.ANY)],
        out_specs=vmem,
        cost_estimate=LIGHT,
        compiler_params=pltpu.CompilerParams(vmem_limit_bytes=6 * 2**20),
        name="diag_total",
    )(ids, own_sum, mine, other, after)


def far_rows(ids, kids, own, after, at, size):
    count, width = own.shape
    slots = 0 if kids is None else kids.shape[0]
    ahead = 0 if kids is None else kids.shape[1] // 2
    hbm = pl.BlockSpec(memory_space=pl.ANY)
    args = [own] + [x for x in (kids, after) if x is not None]

    def body(ids, *refs):
        out_ref, sems = refs[-2:]
        side = ids[1, 0] // 2
        start = pl.multiple_of(side * (count // 2) + at, 256)
        copies = [
            pltpu.make_async_copy(
                refs[0].at[pl.ds(start, size)], out_ref.at[pl.ds(slots * ahead, size)], sems.at[slots]
            )
        ]
        for k in range(slots):
            first = pl.multiple_of(side * ahead, ahead)
            copies.append(
                pltpu.make_async_copy(
                    refs[1].at[k, pl.ds(first, ahead)], out_ref.at[pl.ds(k * ahead, ahead)], sems.at[k]
                )
            )
        for copy in copies:
            copy.start()
        for copy in copies:
            copy.wait()

    return pl.pallas_call(
        body,
        out_shape=jax.ShapeDtypeStruct((slots * ahead + size, width), jnp.float32),
        in_specs=[pl.BlockSpec(memory_space=pltpu.SMEM)] + [hbm] * len(args),
        out_specs=pl.BlockSpec(memory_space=pltpu.VMEM),
        scratch_shapes=[pltpu.SemaphoreType.DMA((slots + 1,))],
        compiler_params=pltpu.CompilerParams(vmem_limit_bytes=6 * 2**20),
        cost_estimate=LIGHT,
        name="far_rows",
    )(ids, *args)


def shards(own_rows, child_blocks, child_parent, child_live, child_first):
    front_id = lax.axis_index("front")
    row_id = lax.axis_index("row")
    col_id = lax.axis_index("col")
    side = col_id // 2
    nfront, nrow = lax.axis_size("front"), lax.axis_size("row")
    here = jnp.stack([front_id, row_id, col_id, col_id]).astype(jnp.int32).reshape(2, 2)
    ids = jnp.concatenate([here, child_live, child_first, child_parent], axis=0)
    own = own_rows[0]
    own_count = own.shape[0]
    slots, child_rows, width = child_blocks.shape[1:]
    across = [(c, c ^ 2) for c in range(4)]
    beside = [(c, c ^ 1) for c in range(4)]

    def ring_send(blocks):
        n = blocks.shape[0]
        quarters = blocks.reshape(n, nrow, width // nrow, width)
        parts = [lax.dynamic_index_in_dim(quarters, row_id, 1, keepdims=False)]
        for s in range(1, nrow):
            piece = lax.dynamic_index_in_dim(quarters, (row_id + s) % nrow, 1, keepdims=False)
            parts.append(lax.ppermute(piece, "row", [(i, (i + s) % nrow) for i in range(nrow)]))
        return parts

    def ring_gather(piece):
        parts = [piece]
        for s in range(1, nrow):
            parts.append(lax.ppermute(piece, "row", [(i, (i + s) % nrow) for i in range(nrow)]))
        return parts

    half_front = nfront // 2
    hi, lo = front_id // half_front, front_id % half_front
    twin = [(f, (f + half_front) % nfront) for f in range(nfront)]

    def x_ring(pieces):
        parts = [pieces[0]]
        for s in range(1, half_front):
            perm = [
                (h * half_front + i, h * half_front + (i + s) % half_front) for h in range(2) for i in range(half_front)
            ]
            parts.append(lax.ppermute(pieces[s], "front", perm))
        return parts

    def from_twin(mine):
        return lax.ppermute(lax.dynamic_index_in_dim(mine, 1 - hi, 0, keepdims=False), "front", twin)

    kids = child_blocks[0].reshape(slots * child_rows, width)
    kid_half = slots * child_rows // 2
    half = own_count // 2
    cut = half // 2
    kid_near = lax.ppermute(kids, "col", beside)
    own_near = lax.ppermute(own, "col", beside)
    send = far_rows(here, child_blocks[0], own, None, 0, cut)
    got = [lax.ppermute(send, "col", across)]

    kid_diag = kid_gram(ids, nfront, slots, kids, kids, kid_near, False, send)
    got.append(lax.ppermute(far_rows(here, None, own, kid_diag, cut, half - cut), "col", across))
    rows = 1024
    own_diag = gram(ids, own, own, own_near, (1, own_count // rows), rows, lambda ids, b: 0, after=kid_diag)
    both = jnp.concatenate([kid_diag.reshape(slots * 2, width, width), own_diag[0]])
    diag_pieces, own_sum = route(ids, slots, nfront, ring_send(both), ids)
    kid_cross = kid_gram(ids, nfront, slots, got[0], kids, kid_near, True, own_diag)
    cross_parts = ring_send(kid_cross.reshape(slots * 2, width, width))
    rows = 512
    half_at, cut_at = half // rows, cut // rows
    cross = gram(
        ids, got[0], own, own_near, (1, cut_at), rows, lambda ids, b: (1 - ids[1, 0] // 2) * half_at,
        after=kid_cross, x_at=kid_half // rows,
    )
    diag_mine = add_parts(x_ring(diag_pieces), cross)
    cross_pieces, _ = route(ids, slots, nfront, cross_parts, diag_mine)
    cross = gram(
        ids, got[1], own, own_near, (1, half_at - cut_at), rows,
        lambda ids, b: (1 - ids[1, 0] // 2) * half_at + cut_at, flip=True, start=cross, after=diag_mine,
    )
    diag = diag_total(ids, half_front, own_sum, diag_mine, from_twin(diag_mine), cross)
    left = jnp.where(side == 0, diag, lax.ppermute(diag, "col", [(0, 2), (1, 3)]))
    cross = add_parts(ring_send(cross[0]), left)
    cross_mine = add_parts(x_ring(cross_pieces), cross)
    kid_cross_sum = lax.dynamic_index_in_dim(cross_mine, hi, 0, keepdims=False) + from_twin(cross_mine)
    aa = jnp.stack(ring_gather(left))
    aa_other = lax.ppermute(aa, "col", beside)

    cross = cross + kid_cross_sum
    same = lax.ppermute(cross[0], "col", [(0, 2), (1, 3)])
    swap = lax.ppermute(cross[1], "col", [(0, 3), (1, 2)])
    right = jnp.concatenate([cross + jnp.stack([same, swap]), diag])
    r_aa, m_aa = head(ids, aa, aa_other, right)
    right = joined(ring_gather(right), m_aa)
    out = tail(ids, r_aa, m_aa, right, lax.ppermute(right, "col", beside))
    return out[None]


def solution(mesh):
    in_specs = (P("front", "row", "col"), P("front", None, "row", "col"), P(), P(), P())
    out_specs = P("front", "row", "col")
    return jax.shard_map(shards, mesh=mesh, in_specs=in_specs, out_specs=out_specs, check_vma=False)
```

```python
import jax
import jax.numpy as jnp
from jax import lax
from jax.experimental import pallas as pl
from jax.experimental.pallas import tpu as pltpu
from jax.sharding import PartitionSpec as P

PANEL = 64
NB = 128
SUB = 8
LIGHT = pl.CostEstimate(flops=1000, bytes_accessed=1000, transcendentals=0)


def spread(x):
    return jnp.broadcast_to(x, (SUB, NB))


def column(strip, at):
    return spread(strip[:, at:at + 1])


def diag_factor(block):
    rows = lax.broadcasted_iota(jnp.int32, (SUB, NB), 0)
    lanes = lax.broadcasted_iota(jnp.int32, (SUB, NB), 1)
    count = NB // SUB
    both = [block[SUB * s:SUB * (s + 1), :] for s in range(count)]
    factor, inverse = [], []
    def read(t, at):
        return [column(both[t], at + k) for k in range(SUB)] if t < count else []

    cols, first, second = read(0, 0), read(1, 0), read(2, 0)
    for s in range(count):
        at = SUB * s
        left = both[s]
        right = jnp.where(lanes < at, left, jnp.where(lanes == rows + at, 1.0, 0.0))
        ahead, ahead_first = read(s + 1, at + SUB), read(s + 2, at + SUB)
        done = lanes < at + SUB
        band = jnp.logical_and(lanes >= at, done)
        sources = []
        for k in range(SUB):
            masked = jnp.where(rows > k, cols[k], 0.0)
            rs = lax.rsqrt(spread(cols[k][k:k + 1, :]))
            m = masked * rs
            lrow = spread(left[k:k + 1, :]) * rs
            rrow = spread(right[k:k + 1, :]) * rs
            sources.append(jnp.where(done, rrow, lrow))
            left = jnp.where(rows == k, lrow, left - m * lrow)
            right = jnp.where(rows == k, rrow, right - m * rrow)
            for panel in (first, second):
                if panel:
                    panel[k] = panel[k] * rs
            for l in range(k + 1, SUB):
                head = spread(cols[l][k:k + 1, :]) * rs
                cols[l] = cols[l] - m * head
                for panel in (first, second):
                    if panel:
                        panel[l] = panel[l] - panel[k] * head
            if first:
                for l in range(SUB):
                    scale = spread(first[k][l:l + 1, :])
                    ahead[l] = ahead[l] - first[k] * scale
                    if second:
                        ahead_first[l] = ahead_first[l] - second[k] * scale
        factor.append(jnp.where(lanes >= rows + at, left, 0.0))
        inverse.append(right)
        for t, panel in ((s + 1, first), (s + 2, second)):
            if panel:
                both[t] = jnp.where(band, 0.0, both[t])
                for k in range(SUB):
                    both[t] = both[t] - panel[k] * sources[k]
        if s + 3 < count:
            source = split(jnp.where(done, right, left))
            update = mul(split(factor[s]), source, 0)
            for t in range(s + 3, count):
                both[t] = jnp.where(band, 0.0, both[t]) - update[SUB * t:SUB * (t + 1), :]
        cols, first, second = ahead, ahead_first, read(s + 3, at + SUB)
    return jnp.concatenate(factor, 0), jnp.concatenate(inverse, 0)


def split(value):
    high = value.astype(jnp.bfloat16)
    return high, (value - high.astype(jnp.float32)).astype(jnp.bfloat16)


def mul(x, y, contract):
    d = lambda p, q: lax.dot_general(p, q, (((contract,), (0,)), ((), ())), preferred_element_type=jnp.float32)
    return d(x[0], y[0]) + (d(x[0], y[1]) + d(x[1], y[0]))


def eliminate(work, inv):
    n = work.shape[0]
    for at in range(0, n, NB):
        here, past = slice(at, at + NB), slice(at + NB, n)
        r, m = diag_factor(work[here, here])
        work[here, here] = r
        ms = split(m)
        more = at + NB < n
        if more:
            row = mul(ms, split(work[here, past]), 1)
            work[here, past] = row
            rows = split(row)
        if inv is not None:
            if at:
                inv[here, :at] = mul(ms, split(inv[here, :at]), 1)
            inv[here, here] = m
        if more:
            for t in range(at + NB, n, NB):
                lhs = tuple(x[:, t - at - NB:t - at] for x in rows)
                rhs = tuple(x[:, t - at - NB:] for x in rows)
                work[t:t + NB, t:] = work[t:t + NB, t:] - mul(lhs, rhs, 0)
            if inv is not None:
                es = split(inv[here, :at + NB])
                inv[past, :at + NB] = inv[past, :at + NB] - mul(rows, es, 0)


def upper(x):
    return jnp.where(
        lax.broadcasted_iota(jnp.int32, x.shape, 1) >= lax.broadcasted_iota(jnp.int32, x.shape, 0), x, 0.0
    )


def place(ref, ids, mine, other, first=0):
    ring, _, part, width = mine.shape
    r, k = ids[0, 1], lax.rem(ids[1, 0], 2)
    for source, core in ((mine, k), (other, 1 - k)):
        for s in range(ring):
            q = lax.rem(r - s + ring, ring)
            at = pl.ds(pl.multiple_of(core * width + q * part, part), part)
            ref[at, pl.ds(pl.multiple_of(core * width, width), width)] = source[s, first]
            ref[at, pl.ds(pl.multiple_of((1 - core) * width, width), width)] = source[s, first + 1]


def head_kernel(ids, mine, other, after, r_ref, m_ref):
    place(r_ref, ids, mine, other)
    m_ref[...] = jnp.zeros_like(m_ref)
    eliminate(r_ref, m_ref)
    r_ref[...] = upper(r_ref[...])


def head(ids, mine, other, after):
    n = 2 * mine.shape[-1]
    vmem = pl.BlockSpec(memory_space=pltpu.VMEM)
    return pl.pallas_call(
        head_kernel,
        out_shape=(jax.ShapeDtypeStruct((n, n), jnp.float32),) * 2,
        in_specs=[pl.BlockSpec(memory_space=pltpu.SMEM), vmem, vmem, pl.BlockSpec(memory_space=pl.ANY)],
        out_specs=(vmem, vmem),
        compiler_params=pltpu.CompilerParams(vmem_limit_bytes=16 * 2**20),
        cost_estimate=pl.CostEstimate(flops=20 * 10**9, bytes_accessed=4 * n * n * 4, transcendentals=0),
        name="head_factor",
    )(ids, mine, other, after)


def tail_kernel(ids, r_aa, m_aa, mine, other, out_ref, ab, bb):
    width = out_ref.shape[0]
    place(ab, ids, mine, other)
    place(bb, ids, mine, other, 2)
    ab[...] = mul(split(m_aa[...]), split(ab[...]), 1)
    cross = split(ab[...])
    bb[...] = bb[...] - mul(cross, cross, 0)
    eliminate(bb, None)
    bb[...] = upper(bb[...])
    r, k, right = ids[0, 1], lax.rem(ids[1, 0], 2), ids[1, 0] // 2
    rows = pl.ds(pl.multiple_of(lax.rem(r, 2) * width, width), width)
    cols = pl.ds(pl.multiple_of(k * width, width), width)
    top = r < 2

    @pl.when(jnp.logical_and(top, right == 0))
    def _():
        out_ref[...] = r_aa[rows, cols]

    @pl.when(jnp.logical_and(top, right == 1))
    def _():
        out_ref[...] = ab[rows, cols]

    @pl.when(jnp.logical_and(jnp.logical_not(top), right == 0))
    def _():
        out_ref[...] = jnp.zeros_like(out_ref)

    @pl.when(jnp.logical_and(jnp.logical_not(top), right == 1))
    def _():
        out_ref[...] = bb[rows, cols]


def tail(ids, r_aa, m_aa, mine, other):
    n = r_aa.shape[0]
    vmem = pl.BlockSpec(memory_space=pltpu.VMEM)
    return pl.pallas_call(
        tail_kernel,
        out_shape=jax.ShapeDtypeStruct((n // 2, n // 2), jnp.float32),
        in_specs=[pl.BlockSpec(memory_space=pltpu.SMEM)] + [vmem] * 4,
        out_specs=vmem,
        scratch_shapes=[pltpu.VMEM((n, n), jnp.float32)] * 2,
        compiler_params=pltpu.CompilerParams(vmem_limit_bytes=16 * 2**20),
        cost_estimate=LIGHT,
        name="tail_factor",
    )(ids, r_aa, m_aa, mine, other)


def sides(ids):
    return ids[1, 0] // 2, lax.rem(ids[1, 0], 2)


def part(x, y):
    return lax.dot_general(x, y, (((0,), (0,)), ((), ())), preferred_element_type=jnp.float32)


def add_products(out_ref, x, ys):
    xh, xl = split(x)
    for i, ref in enumerate(ys):
        yh, yl = split(ref[...])
        out_ref[0, i] += part(xh, yh) + (part(xh, yl) + part(xl, yh))


def gram_kernel(flip, ids, x_ref, y0_ref, y1_ref, start_ref, after, out_ref):
    step = pl.program_id(1)

    @pl.when(step == 0)
    def _():
        out_ref[...] = jnp.zeros_like(out_ref) if start_ref is None else start_ref[...]

    add_products(out_ref, x_ref[...], (y0_ref, y1_ref))
    if flip:

        @pl.when(jnp.logical_and(step == pl.num_programs(1) - 1, sides(ids)[0] == 0))
        def _():
            for i in range(2):
                out_ref[0, i] = out_ref[0, i].T


def kid_kernel(far, fronts, slots, ids, x_ref, y0_ref, y1_ref, after, out_ref):
    kid = pl.program_id(0)
    side, core = sides(ids)
    rows, width = x_ref.shape
    base = ids[0, 1] * (2 * rows) + (1 - side) * rows if far else ids[0, 1] * rows
    inside = lax.broadcasted_iota(jnp.int32, (rows, width), 0) + base < ids[2 + ids[0, 0], kid]
    out_ref[...] = jnp.zeros_like(out_ref)
    add_products(out_ref, jnp.where(inside, x_ref[...], 0.0), (y0_ref, y1_ref))
    edge = ids[2 + fronts + ids[0, 0], kid] * PANEL
    left = 2 * (1 - side) + core if far else ids[1, 0]
    for i in range(2):
        right = 2 * side + (core if i == 0 else 1 - core)
        keep = jnp.logical_and(
            lax.broadcasted_iota(jnp.int32, (width, width), 0) + left * width >= edge,
            lax.broadcasted_iota(jnp.int32, (width, width), 1) + right * width >= edge,
        )
        out_ref[0, i] = jnp.where(keep, out_ref[0, i], 0.0)
    if far:

        @pl.when(side == 0)
        def _():
            for i in range(2):
                out_ref[0, i] = out_ref[0, i].T


def gram(ids, x, y0, y1, grid, rows, y_at, flip=False, start=None, after=None, x_at=0):
    width = x.shape[1]
    batch, steps = grid
    xspec = pl.BlockSpec((rows, width), lambda b, i, ids: (x_at + b * steps + i, 0))
    yspec = pl.BlockSpec((rows, width), lambda b, i, ids: (y_at(ids, b) + i, 0))
    ospec = pl.BlockSpec((1, 2, width, width), lambda b, i, ids: (b, 0, 0, 0))
    args, specs = [x, y0, y1], [xspec, yspec, yspec]
    if start is not None:
        args.append(start)
        specs.append(ospec)
    if after is not None:
        args.append(after)
        specs.append(pl.BlockSpec(memory_space=pl.ANY))

    def body(ids, x_ref, y0_ref, y1_ref, *rest):
        gram_kernel(flip, ids, x_ref, y0_ref, y1_ref, None if start is None else rest[0], None, rest[-1])

    return pl.pallas_call(
        body,
        out_shape=jax.ShapeDtypeStruct((batch, 2, width, width), jnp.float32),
        grid_spec=pltpu.PrefetchScalarGridSpec(num_scalar_prefetch=1, grid=grid, in_specs=specs, out_specs=ospec),
        compiler_params=pltpu.CompilerParams(vmem_limit_bytes=16 * 2**20),
        cost_estimate=LIGHT,
        name="own_products",
    )(ids, *args)


def kid_gram(ids, fronts, slots, x, y0, y1, far, after):
    rows, width = y0.shape[0] // slots // (2 if far else 1), x.shape[1]
    xspec = pl.BlockSpec((rows, width), lambda b, ids: (b, 0))
    yspec = pl.BlockSpec((rows, width), lambda b, ids: (2 * b + 1 - ids[1, 0] // 2, 0)) if far else xspec

    def body(ids, x_ref, y0_ref, y1_ref, after_ref, out_ref):
        kid_kernel(far, fronts, slots, ids, x_ref, y0_ref, y1_ref, after_ref, out_ref)

    return pl.pallas_call(
        body,
        out_shape=jax.ShapeDtypeStruct((slots, 2, width, width), jnp.float32),
        grid_spec=pltpu.PrefetchScalarGridSpec(
            num_scalar_prefetch=1,
            grid=(slots,),
            in_specs=[xspec, yspec, yspec, pl.BlockSpec(memory_space=pl.ANY)],
            out_specs=pl.BlockSpec((1, 2, width, width), lambda b, ids: (b, 0, 0, 0)),
        ),
        compiler_params=pltpu.CompilerParams(vmem_limit_bytes=12 * 2**20),
        cost_estimate=LIGHT,
        name="child_products",
    )(ids, x, y0, y1, after)


def route_kernel(slots, fronts, ids, *refs):
    parts, outs = refs[:4], refs[-5:]
    total = (parts[0][...] + parts[1][...]) + (parts[2][...] + parts[3][...])
    blocks = 2
    half = fronts // 2
    lo = lax.rem(ids[0, 0], half)
    base = 2 + 2 * fronts + ids[0, 0]
    for s in range(half):
        for h in range(2):
            parent = h * half + lax.rem(lo + s, half)
            piece = jnp.zeros_like(total[:blocks])
            for k in range(slots):
                kid = total[k * blocks : (k + 1) * blocks]
                piece = piece + jnp.where(ids[base, k] == parent, kid, 0.0)
            outs[s][h] = piece
    if total.shape[0] > slots * blocks:
        outs[4][...] = total[slots * blocks :]
    else:
        outs[4][...] = jnp.zeros_like(outs[4])


def route(ids, slots, fronts, parts, after):
    part, width = parts[0].shape[1:]
    vmem = pl.BlockSpec(memory_space=pltpu.VMEM)
    piece = jax.ShapeDtypeStruct((2, 2, part, width), jnp.float32)
    rest = jax.ShapeDtypeStruct((2, part, width) if parts[0].shape[0] > 2 * slots else (8, 128), jnp.float32)

    def body(ids, *refs):
        route_kernel(slots, fronts, ids, *refs)

    out = pl.pallas_call(
        body,
        out_shape=(piece,) * 4 + (rest,),
        in_specs=[pl.BlockSpec(memory_space=pltpu.SMEM)] + [vmem] * 4 + [pl.BlockSpec(memory_space=pl.ANY)],
        out_specs=(vmem,) * 5,
        cost_estimate=LIGHT,
        compiler_params=pltpu.CompilerParams(vmem_limit_bytes=8 * 2**20),
        name="child_routes",
    )(ids, *parts, after)
    return out[:4], out[4]


def add_kernel(*refs):
    refs[-1][...] = (refs[0][...] + refs[1][...]) + (refs[2][...] + refs[3][...])


def add_parts(parts, after):
    vmem = pl.BlockSpec(memory_space=pltpu.VMEM)
    return pl.pallas_call(
        add_kernel,
        out_shape=jax.ShapeDtypeStruct(parts[0].shape, jnp.float32),
        in_specs=[vmem] * 4 + [pl.BlockSpec(memory_space=pl.ANY)],
        out_specs=vmem,
        cost_estimate=LIGHT,
        compiler_params=pltpu.CompilerParams(vmem_limit_bytes=6 * 2**20),
        name="ring_total",
    )(*parts, after)


def joined(parts, after):
    vmem = pl.BlockSpec(memory_space=pltpu.VMEM)

    def body(*refs):
        for i, ref in enumerate(refs[: len(parts)]):
            refs[-1][i] = ref[...]

    return pl.pallas_call(
        body,
        out_shape=jax.ShapeDtypeStruct((len(parts),) + parts[0].shape, jnp.float32),
        in_specs=[vmem] * len(parts) + [pl.BlockSpec(memory_space=pl.ANY)],
        out_specs=vmem,
        cost_estimate=LIGHT,
        compiler_params=pltpu.CompilerParams(vmem_limit_bytes=6 * 2**20),
        name="ring_parts",
    )(*parts, after)


def diag_total(ids, half_front, own_sum, mine, other, after):
    vmem = pl.BlockSpec(memory_space=pltpu.VMEM)

    def body(ids, own_ref, mine_ref, other_ref, after_ref, out_ref):
        out_ref[...] = own_ref[...] + mine_ref[ids[0, 0] // half_front] + other_ref[...]

    return pl.pallas_call(
        body,
        out_shape=jax.ShapeDtypeStruct(own_sum.shape, jnp.float32),
        in_specs=[pl.BlockSpec(memory_space=pltpu.SMEM)] + [vmem] * 3 + [pl.BlockSpec(memory_space=pl.ANY)],
        out_specs=vmem,
        cost_estimate=LIGHT,
        compiler_params=pltpu.CompilerParams(vmem_limit_bytes=6 * 2**20),
        name="diag_total",
    )(ids, own_sum, mine, other, after)


def far_rows(ids, kids, own, after, at, size):
    count, width = own.shape
    slots = 0 if kids is None else kids.shape[0]
    ahead = 0 if kids is None else kids.shape[1] // 2
    hbm = pl.BlockSpec(memory_space=pl.ANY)
    args = [own] + [x for x in (kids, after) if x is not None]

    def body(ids, *refs):
        out_ref, sems = refs[-2:]
        side = ids[1, 0] // 2
        start = pl.multiple_of(side * (count // 2) + at, 256)
        copies = [
            pltpu.make_async_copy(
                refs[0].at[pl.ds(start, size)], out_ref.at[pl.ds(slots * ahead, size)], sems.at[slots]
            )
        ]
        for k in range(slots):
            first = pl.multiple_of(side * ahead, ahead)
            copies.append(
                pltpu.make_async_copy(
                    refs[1].at[k, pl.ds(first, ahead)], out_ref.at[pl.ds(k * ahead, ahead)], sems.at[k]
                )
            )
        for copy in copies:
            copy.start()
        for copy in copies:
            copy.wait()

    return pl.pallas_call(
        body,
        out_shape=jax.ShapeDtypeStruct((slots * ahead + size, width), jnp.float32),
        in_specs=[pl.BlockSpec(memory_space=pltpu.SMEM)] + [hbm] * len(args),
        out_specs=pl.BlockSpec(memory_space=pltpu.VMEM),
        scratch_shapes=[pltpu.SemaphoreType.DMA((slots + 1,))],
        compiler_params=pltpu.CompilerParams(vmem_limit_bytes=6 * 2**20),
        cost_estimate=LIGHT,
        name="far_rows",
    )(ids, *args)


def shards(own_rows, child_blocks, child_parent, child_live, child_first):
    front_id = lax.axis_index("front")
    row_id = lax.axis_index("row")
    col_id = lax.axis_index("col")
    side = col_id // 2
    nfront, nrow = lax.axis_size("front"), lax.axis_size("row")
    here = jnp.stack([front_id, row_id, col_id, col_id]).astype(jnp.int32).reshape(2, 2)
    ids = jnp.concatenate([here, child_live, child_first, child_parent], axis=0)
    own = own_rows[0]
    own_count = own.shape[0]
    slots, child_rows, width = child_blocks.shape[1:]
    across = [(c, c ^ 2) for c in range(4)]
    beside = [(c, c ^ 1) for c in range(4)]

    def ring_send(blocks):
        n = blocks.shape[0]
        quarters = blocks.reshape(n, nrow, width // nrow, width)
        parts = [lax.dynamic_index_in_dim(quarters, row_id, 1, keepdims=False)]
        for s in range(1, nrow):
            piece = lax.dynamic_index_in_dim(quarters, (row_id + s) % nrow, 1, keepdims=False)
            parts.append(lax.ppermute(piece, "row", [(i, (i + s) % nrow) for i in range(nrow)]))
        return parts

    def ring_gather(piece):
        parts = [piece]
        for s in range(1, nrow):
            parts.append(lax.ppermute(piece, "row", [(i, (i + s) % nrow) for i in range(nrow)]))
        return parts

    half_front = nfront // 2
    hi, lo = front_id // half_front, front_id % half_front
    twin = [(f, (f + half_front) % nfront) for f in range(nfront)]

    def x_ring(pieces):
        parts = [pieces[0]]
        for s in range(1, half_front):
            perm = [
                (h * half_front + i, h * half_front + (i + s) % half_front) for h in range(2) for i in range(half_front)
            ]
            parts.append(lax.ppermute(pieces[s], "front", perm))
        return parts

    def from_twin(mine):
        return lax.ppermute(lax.dynamic_index_in_dim(mine, 1 - hi, 0, keepdims=False), "front", twin)

    kids = child_blocks[0].reshape(slots * child_rows, width)
    kid_half = slots * child_rows // 2
    half = own_count // 2
    cut = half // 2
    kid_near = lax.ppermute(kids, "col", beside)
    own_near = lax.ppermute(own, "col", beside)
    got = [lax.ppermute(lax.dynamic_slice_in_dim(own, side * half, cut, 0), "col", across)]
    kid_send = lax.dynamic_slice_in_dim(child_blocks[0], side * (child_rows // 2), child_rows // 2, 1)
    got_kids = lax.ppermute(kid_send.reshape(kid_half, width), "col", across)

    kid_diag = kid_gram(ids, nfront, slots, kids, kids, kid_near, False, ids)
    got.append(lax.ppermute(far_rows(here, None, own, kid_diag, cut, half - cut), "col", across))
    rows = 1024
    own_diag = gram(ids, own, own, own_near, (1, own_count // rows), rows, lambda ids, b: 0, after=kid_diag)
    diag_pieces, _ = route(ids, slots, nfront, ring_send(kid_diag.reshape(slots * 2, width, width)), own_diag)
    own_sum = add_parts(ring_send(own_diag[0]), ids)
    kid_cross = kid_gram(ids, nfront, slots, got_kids, kids, kid_near, True, diag_pieces[1])
    cross_parts = ring_send(kid_cross.reshape(slots * 2, width, width))
    rows = 512
    half_at, cut_at = half // rows, cut // rows
    cross = gram(
        ids, got[0], own, own_near, (1, cut_at), rows, lambda ids, b: (1 - ids[1, 0] // 2) * half_at,
        after=own_sum,
    )
    diag_mine = add_parts(x_ring(diag_pieces), cross)
    cross_pieces, _ = route(ids, slots, nfront, cross_parts, diag_mine)
    cross = gram(
        ids, got[1], own, own_near, (1, half_at - cut_at), rows,
        lambda ids, b: (1 - ids[1, 0] // 2) * half_at + cut_at, flip=True, start=cross, after=diag_mine,
    )
    diag = diag_total(ids, half_front, own_sum, diag_mine, from_twin(diag_mine), cross)
    left = jnp.where(side == 0, diag, lax.ppermute(diag, "col", [(0, 2), (1, 3)]))
    cross = add_parts(ring_send(cross[0]), left)
    cross_mine = add_parts(x_ring(cross_pieces), cross)
    kid_cross_sum = lax.dynamic_index_in_dim(cross_mine, hi, 0, keepdims=False) + from_twin(cross_mine)
    aa = jnp.stack(ring_gather(left))
    aa_other = lax.ppermute(aa, "col", beside)

    cross = cross + kid_cross_sum
    same = lax.ppermute(cross[0], "col", [(0, 2), (1, 3)])
    swap = lax.ppermute(cross[1], "col", [(0, 3), (1, 2)])
    right = jnp.concatenate([cross + jnp.stack([same, swap]), diag])
    r_aa, m_aa = head(ids, aa, aa_other, right)
    right = joined(ring_gather(right), m_aa)
    out = tail(ids, r_aa, m_aa, right, lax.ppermute(right, "col", beside))
    return out[None]


def solution(mesh):
    in_specs = (P("front", "row", "col"), P("front", None, "row", "col"), P(), P(), P())
    out_specs = P("front", "row", "col")
    return jax.shard_map(shards, mesh=mesh, in_specs=in_specs, out_specs=out_specs, check_vma=False)
```

```python
import jax
import jax.numpy as jnp
from jax import lax
from jax.experimental import pallas as pl
from jax.experimental.pallas import tpu as pltpu
from jax.sharding import PartitionSpec as P

PANEL = 64
NB = 128
SUB = 8
LIGHT = pl.CostEstimate(flops=1000, bytes_accessed=1000, transcendentals=0)


def spread(x):
    return jnp.broadcast_to(x, (SUB, NB))


def column(strip, at):
    return spread(strip[:, at:at + 1])


def diag_factor(block):
    rows = lax.broadcasted_iota(jnp.int32, (SUB, NB), 0)
    lanes = lax.broadcasted_iota(jnp.int32, (SUB, NB), 1)
    count = NB // SUB
    both = [block[SUB * s:SUB * (s + 1), :] for s in range(count)]
    factor, inverse = [], []
    def read(t, at):
        return [column(both[t], at + k) for k in range(SUB)] if t < count else []

    cols, first, second = read(0, 0), read(1, 0), read(2, 0)
    for s in range(count):
        at = SUB * s
        left = both[s]
        right = jnp.where(lanes < at, left, jnp.where(lanes == rows + at, 1.0, 0.0))
        ahead, ahead_first = read(s + 1, at + SUB), read(s + 2, at + SUB)
        done = lanes < at + SUB
        band = jnp.logical_and(lanes >= at, done)
        sources = []
        for k in range(SUB):
            masked = jnp.where(rows > k, cols[k], 0.0)
            rs = lax.rsqrt(spread(cols[k][k:k + 1, :]))
            m = masked * rs
            lrow = spread(left[k:k + 1, :]) * rs
            rrow = spread(right[k:k + 1, :]) * rs
            sources.append(jnp.where(done, rrow, lrow))
            left = jnp.where(rows == k, lrow, left - m * lrow)
            right = jnp.where(rows == k, rrow, right - m * rrow)
            for panel in (first, second):
                if panel:
                    panel[k] = panel[k] * rs
            for l in range(k + 1, SUB):
                head = spread(cols[l][k:k + 1, :]) * rs
                cols[l] = cols[l] - m * head
                for panel in (first, second):
                    if panel:
                        panel[l] = panel[l] - panel[k] * head
            if first:
                for l in range(SUB):
                    scale = spread(first[k][l:l + 1, :])
                    ahead[l] = ahead[l] - first[k] * scale
                    if second:
                        ahead_first[l] = ahead_first[l] - second[k] * scale
        factor.append(jnp.where(lanes >= rows + at, left, 0.0))
        inverse.append(right)
        for t, panel in ((s + 1, first), (s + 2, second)):
            if panel:
                both[t] = jnp.where(band, 0.0, both[t])
                for k in range(SUB):
                    both[t] = both[t] - panel[k] * sources[k]
        if s + 3 < count:
            source = split(jnp.where(done, right, left))
            update = mul(split(factor[s]), source, 0)
            for t in range(s + 3, count):
                both[t] = jnp.where(band, 0.0, both[t]) - update[SUB * t:SUB * (t + 1), :]
        cols, first, second = ahead, ahead_first, read(s + 3, at + SUB)
    return jnp.concatenate(factor, 0), jnp.concatenate(inverse, 0)


def split(value):
    high = value.astype(jnp.bfloat16)
    return high, (value - high.astype(jnp.float32)).astype(jnp.bfloat16)


def mul(x, y, contract):
    d = lambda p, q: lax.dot_general(p, q, (((contract,), (0,)), ((), ())), preferred_element_type=jnp.float32)
    return d(x[0], y[0]) + (d(x[0], y[1]) + d(x[1], y[0]))


def eliminate(work, inv):
    n = work.shape[0]
    for at in range(0, n, NB):
        here, past = slice(at, at + NB), slice(at + NB, n)
        r, m = diag_factor(work[here, here])
        work[here, here] = r
        ms = split(m)
        more = at + NB < n
        if more:
            row = mul(ms, split(work[here, past]), 1)
            work[here, past] = row
            rows = split(row)
        if inv is not None:
            if at:
                inv[here, :at] = mul(ms, split(inv[here, :at]), 1)
            inv[here, here] = m
        if more:
            for t in range(at + NB, n, NB):
                lhs = tuple(x[:, t - at - NB:t - at] for x in rows)
                rhs = tuple(x[:, t - at - NB:] for x in rows)
                work[t:t + NB, t:] = work[t:t + NB, t:] - mul(lhs, rhs, 0)
            if inv is not None:
                es = split(inv[here, :at + NB])
                inv[past, :at + NB] = inv[past, :at + NB] - mul(rows, es, 0)


def upper(x):
    return jnp.where(
        lax.broadcasted_iota(jnp.int32, x.shape, 1) >= lax.broadcasted_iota(jnp.int32, x.shape, 0), x, 0.0
    )


def place(ref, ids, mine, other, first=0):
    ring, _, part, width = mine.shape
    r, k = ids[0, 1], lax.rem(ids[1, 0], 2)
    for source, core in ((mine, k), (other, 1 - k)):
        for s in range(ring):
            q = lax.rem(r - s + ring, ring)
            at = pl.ds(pl.multiple_of(core * width + q * part, part), part)
            ref[at, pl.ds(pl.multiple_of(core * width, width), width)] = source[s, first]
            ref[at, pl.ds(pl.multiple_of((1 - core) * width, width), width)] = source[s, first + 1]


def head_kernel(ids, mine, other, after, r_ref, m_ref):
    place(r_ref, ids, mine, other)
    m_ref[...] = jnp.zeros_like(m_ref)
    eliminate(r_ref, m_ref)
    r_ref[...] = upper(r_ref[...])


def head(ids, mine, other, after):
    n = 2 * mine.shape[-1]
    vmem = pl.BlockSpec(memory_space=pltpu.VMEM)
    return pl.pallas_call(
        head_kernel,
        out_shape=(jax.ShapeDtypeStruct((n, n), jnp.float32),) * 2,
        in_specs=[pl.BlockSpec(memory_space=pltpu.SMEM), vmem, vmem, pl.BlockSpec(memory_space=pl.ANY)],
        out_specs=(vmem, vmem),
        compiler_params=pltpu.CompilerParams(vmem_limit_bytes=16 * 2**20),
        cost_estimate=pl.CostEstimate(flops=20 * 10**9, bytes_accessed=4 * n * n * 4, transcendentals=0),
        name="head_factor",
    )(ids, mine, other, after)


def tail_kernel(ids, r_aa, m_aa, mine, other, out_ref, ab, bb):
    width = out_ref.shape[0]
    place(ab, ids, mine, other)
    place(bb, ids, mine, other, 2)
    ab[...] = mul(split(m_aa[...]), split(ab[...]), 1)
    cross = split(ab[...])
    bb[...] = bb[...] - mul(cross, cross, 0)
    eliminate(bb, None)
    bb[...] = upper(bb[...])
    r, k, right = ids[0, 1], lax.rem(ids[1, 0], 2), ids[1, 0] // 2
    rows = pl.ds(pl.multiple_of(lax.rem(r, 2) * width, width), width)
    cols = pl.ds(pl.multiple_of(k * width, width), width)
    top = r < 2

    @pl.when(jnp.logical_and(top, right == 0))
    def _():
        out_ref[...] = r_aa[rows, cols]

    @pl.when(jnp.logical_and(top, right == 1))
    def _():
        out_ref[...] = ab[rows, cols]

    @pl.when(jnp.logical_and(jnp.logical_not(top), right == 0))
    def _():
        out_ref[...] = jnp.zeros_like(out_ref)

    @pl.when(jnp.logical_and(jnp.logical_not(top), right == 1))
    def _():
        out_ref[...] = bb[rows, cols]


def tail(ids, r_aa, m_aa, mine, other):
    n = r_aa.shape[0]
    vmem = pl.BlockSpec(memory_space=pltpu.VMEM)
    return pl.pallas_call(
        tail_kernel,
        out_shape=jax.ShapeDtypeStruct((n // 2, n // 2), jnp.float32),
        in_specs=[pl.BlockSpec(memory_space=pltpu.SMEM)] + [vmem] * 4,
        out_specs=vmem,
        scratch_shapes=[pltpu.VMEM((n, n), jnp.float32)] * 2,
        compiler_params=pltpu.CompilerParams(vmem_limit_bytes=16 * 2**20),
        cost_estimate=LIGHT,
        name="tail_factor",
    )(ids, r_aa, m_aa, mine, other)


def sides(ids):
    return ids[1, 0] // 2, lax.rem(ids[1, 0], 2)


def part(x, y):
    return lax.dot_general(x, y, (((0,), (0,)), ((), ())), preferred_element_type=jnp.float32)


def add_products(out_ref, x, ys):
    xh, xl = split(x)
    for i, ref in enumerate(ys):
        yh, yl = split(ref[...])
        out_ref[0, i] += part(xh, yh) + (part(xh, yl) + part(xl, yh))


def gram_kernel(flip, ids, x_ref, y0_ref, y1_ref, start_ref, after, out_ref):
    step = pl.program_id(1)

    @pl.when(step == 0)
    def _():
        out_ref[...] = jnp.zeros_like(out_ref) if start_ref is None else start_ref[...]

    add_products(out_ref, x_ref[...], (y0_ref, y1_ref))
    if flip:

        @pl.when(jnp.logical_and(step == pl.num_programs(1) - 1, sides(ids)[0] == 0))
        def _():
            for i in range(2):
                out_ref[0, i] = out_ref[0, i].T


def kid_kernel(far, fronts, slots, ids, x_ref, y0_ref, y1_ref, after, out_ref):
    kid = pl.program_id(0)
    side, core = sides(ids)
    rows, width = x_ref.shape
    base = ids[0, 1] * (2 * rows) + (1 - side) * rows if far else ids[0, 1] * rows
    inside = lax.broadcasted_iota(jnp.int32, (rows, width), 0) + base < ids[2 + ids[0, 0], kid]
    out_ref[...] = jnp.zeros_like(out_ref)
    add_products(out_ref, jnp.where(inside, x_ref[...], 0.0), (y0_ref, y1_ref))
    edge = ids[2 + fronts + ids[0, 0], kid] * PANEL
    left = 2 * (1 - side) + core if far else ids[1, 0]
    for i in range(2):
        right = 2 * side + (core if i == 0 else 1 - core)
        keep = jnp.logical_and(
            lax.broadcasted_iota(jnp.int32, (width, width), 0) + left * width >= edge,
            lax.broadcasted_iota(jnp.int32, (width, width), 1) + right * width >= edge,
        )
        out_ref[0, i] = jnp.where(keep, out_ref[0, i], 0.0)
    if far:

        @pl.when(side == 0)
        def _():
            for i in range(2):
                out_ref[0, i] = out_ref[0, i].T


def gram(ids, x, y0, y1, grid, rows, y_at, flip=False, start=None, after=None, x_at=0):
    width = x.shape[1]
    batch, steps = grid
    xspec = pl.BlockSpec((rows, width), lambda b, i, ids: (x_at + b * steps + i, 0))
    yspec = pl.BlockSpec((rows, width), lambda b, i, ids: (y_at(ids, b) + i, 0))
    ospec = pl.BlockSpec((1, 2, width, width), lambda b, i, ids: (b, 0, 0, 0))
    args, specs = [x, y0, y1], [xspec, yspec, yspec]
    if start is not None:
        args.append(start)
        specs.append(ospec)
    if after is not None:
        args.append(after)
        specs.append(pl.BlockSpec(memory_space=pl.ANY))

    def body(ids, x_ref, y0_ref, y1_ref, *rest):
        gram_kernel(flip, ids, x_ref, y0_ref, y1_ref, None if start is None else rest[0], None, rest[-1])

    return pl.pallas_call(
        body,
        out_shape=jax.ShapeDtypeStruct((batch, 2, width, width), jnp.float32),
        grid_spec=pltpu.PrefetchScalarGridSpec(num_scalar_prefetch=1, grid=grid, in_specs=specs, out_specs=ospec),
        compiler_params=pltpu.CompilerParams(vmem_limit_bytes=16 * 2**20),
        cost_estimate=LIGHT,
        name="own_products",
    )(ids, *args)


def kid_gram(ids, fronts, slots, x, y0, y1, far, after):
    rows, width = y0.shape[0] // slots // (2 if far else 1), x.shape[1]
    xspec = pl.BlockSpec((rows, width), lambda b, ids: (b, 0))
    yspec = pl.BlockSpec((rows, width), lambda b, ids: (2 * b + 1 - ids[1, 0] // 2, 0)) if far else xspec

    def body(ids, x_ref, y0_ref, y1_ref, after_ref, out_ref):
        kid_kernel(far, fronts, slots, ids, x_ref, y0_ref, y1_ref, after_ref, out_ref)

    return pl.pallas_call(
        body,
        out_shape=jax.ShapeDtypeStruct((slots, 2, width, width), jnp.float32),
        grid_spec=pltpu.PrefetchScalarGridSpec(
            num_scalar_prefetch=1,
            grid=(slots,),
            in_specs=[xspec, yspec, yspec, pl.BlockSpec(memory_space=pl.ANY)],
            out_specs=pl.BlockSpec((1, 2, width, width), lambda b, ids: (b, 0, 0, 0)),
        ),
        compiler_params=pltpu.CompilerParams(vmem_limit_bytes=12 * 2**20),
        cost_estimate=LIGHT,
        name="child_products",
    )(ids, x, y0, y1, after)


def route_kernel(slots, fronts, ids, *refs):
    parts, outs = refs[:4], refs[-5:]
    total = (parts[0][...] + parts[1][...]) + (parts[2][...] + parts[3][...])
    blocks = 2
    half = fronts // 2
    lo = lax.rem(ids[0, 0], half)
    base = 2 + 2 * fronts + ids[0, 0]
    for s in range(half):
        for h in range(2):
            parent = h * half + lax.rem(lo + s, half)
            piece = jnp.zeros_like(total[:blocks])
            for k in range(slots):
                kid = total[k * blocks : (k + 1) * blocks]
                piece = piece + jnp.where(ids[base, k] == parent, kid, 0.0)
            outs[s][h] = piece
    if total.shape[0] > slots * blocks:
        outs[4][...] = total[slots * blocks :]
    else:
        outs[4][...] = jnp.zeros_like(outs[4])


def route(ids, slots, fronts, parts, after):
    part, width = parts[0].shape[1:]
    vmem = pl.BlockSpec(memory_space=pltpu.VMEM)
    piece = jax.ShapeDtypeStruct((2, 2, part, width), jnp.float32)
    rest = jax.ShapeDtypeStruct((2, part, width) if parts[0].shape[0] > 2 * slots else (8, 128), jnp.float32)

    def body(ids, *refs):
        route_kernel(slots, fronts, ids, *refs)

    out = pl.pallas_call(
        body,
        out_shape=(piece,) * 4 + (rest,),
        in_specs=[pl.BlockSpec(memory_space=pltpu.SMEM)] + [vmem] * 4 + [pl.BlockSpec(memory_space=pl.ANY)],
        out_specs=(vmem,) * 5,
        cost_estimate=LIGHT,
        compiler_params=pltpu.CompilerParams(vmem_limit_bytes=8 * 2**20),
        name="child_routes",
    )(ids, *parts, after)
    return out[:4], out[4]


def add_kernel(*refs):
    refs[-1][...] = (refs[0][...] + refs[1][...]) + (refs[2][...] + refs[3][...])


def add_parts(parts, after):
    vmem = pl.BlockSpec(memory_space=pltpu.VMEM)
    return pl.pallas_call(
        add_kernel,
        out_shape=jax.ShapeDtypeStruct(parts[0].shape, jnp.float32),
        in_specs=[vmem] * 4 + [pl.BlockSpec(memory_space=pl.ANY)],
        out_specs=vmem,
        cost_estimate=LIGHT,
        compiler_params=pltpu.CompilerParams(vmem_limit_bytes=6 * 2**20),
        name="ring_total",
    )(*parts, after)


def joined(parts, after):
    vmem = pl.BlockSpec(memory_space=pltpu.VMEM)

    def body(*refs):
        for i, ref in enumerate(refs[: len(parts)]):
            refs[-1][i] = ref[...]

    return pl.pallas_call(
        body,
        out_shape=jax.ShapeDtypeStruct((len(parts),) + parts[0].shape, jnp.float32),
        in_specs=[vmem] * len(parts) + [pl.BlockSpec(memory_space=pl.ANY)],
        out_specs=vmem,
        cost_estimate=LIGHT,
        compiler_params=pltpu.CompilerParams(vmem_limit_bytes=6 * 2**20),
        name="ring_parts",
    )(*parts, after)


def diag_total(ids, half_front, own_sum, mine, other, after):
    vmem = pl.BlockSpec(memory_space=pltpu.VMEM)

    def body(ids, own_ref, mine_ref, other_ref, after_ref, out_ref):
        out_ref[...] = own_ref[...] + mine_ref[ids[0, 0] // half_front] + other_ref[...]

    return pl.pallas_call(
        body,
        out_shape=jax.ShapeDtypeStruct(own_sum.shape, jnp.float32),
        in_specs=[pl.BlockSpec(memory_space=pltpu.SMEM)] + [vmem] * 3 + [pl.BlockSpec(memory_space=pl.ANY)],
        out_specs=vmem,
        cost_estimate=LIGHT,
        compiler_params=pltpu.CompilerParams(vmem_limit_bytes=6 * 2**20),
        name="diag_total",
    )(ids, own_sum, mine, other, after)


def far_rows(ids, kids, own, after, at, size):
    count, width = own.shape
    slots = 0 if kids is None else kids.shape[0]
    ahead = 0 if kids is None else kids.shape[1] // 2
    hbm = pl.BlockSpec(memory_space=pl.ANY)
    args = [own] + [x for x in (kids, after) if x is not None]

    def body(ids, *refs):
        out_ref, sems = refs[-2:]
        side = ids[1, 0] // 2
        start = pl.multiple_of(side * (count // 2) + at, 256)
        copies = [
            pltpu.make_async_copy(
                refs[0].at[pl.ds(start, size)], out_ref.at[pl.ds(slots * ahead, size)], sems.at[slots]
            )
        ]
        for k in range(slots):
            first = pl.multiple_of(side * ahead, ahead)
            copies.append(
                pltpu.make_async_copy(
                    refs[1].at[k, pl.ds(first, ahead)], out_ref.at[pl.ds(k * ahead, ahead)], sems.at[k]
                )
            )
        for copy in copies:
            copy.start()
        for copy in copies:
            copy.wait()

    return pl.pallas_call(
        body,
        out_shape=jax.ShapeDtypeStruct((slots * ahead + size, width), jnp.float32),
        in_specs=[pl.BlockSpec(memory_space=pltpu.SMEM)] + [hbm] * len(args),
        out_specs=pl.BlockSpec(memory_space=pltpu.VMEM),
        scratch_shapes=[pltpu.SemaphoreType.DMA((slots + 1,))],
        compiler_params=pltpu.CompilerParams(vmem_limit_bytes=6 * 2**20),
        cost_estimate=LIGHT,
        name="far_rows",
    )(ids, *args)


def shards(own_rows, child_blocks, child_parent, child_live, child_first):
    front_id = lax.axis_index("front")
    row_id = lax.axis_index("row")
    col_id = lax.axis_index("col")
    side = col_id // 2
    nfront, nrow = lax.axis_size("front"), lax.axis_size("row")
    here = jnp.stack([front_id, row_id, col_id, col_id]).astype(jnp.int32).reshape(2, 2)
    ids = jnp.concatenate([here, child_live, child_first, child_parent], axis=0)
    own = own_rows[0]
    own_count = own.shape[0]
    slots, child_rows, width = child_blocks.shape[1:]
    across = [(c, c ^ 2) for c in range(4)]
    beside = [(c, c ^ 1) for c in range(4)]

    def ring_send(blocks):
        n = blocks.shape[0]
        quarters = blocks.reshape(n, nrow, width // nrow, width)
        parts = [lax.dynamic_index_in_dim(quarters, row_id, 1, keepdims=False)]
        for s in range(1, nrow):
            piece = lax.dynamic_index_in_dim(quarters, (row_id + s) % nrow, 1, keepdims=False)
            parts.append(lax.ppermute(piece, "row", [(i, (i + s) % nrow) for i in range(nrow)]))
        return parts

    def ring_gather(piece):
        parts = [piece]
        for s in range(1, nrow):
            parts.append(lax.ppermute(piece, "row", [(i, (i + s) % nrow) for i in range(nrow)]))
        return parts

    half_front = nfront // 2
    hi, lo = front_id // half_front, front_id % half_front
    twin = [(f, (f + half_front) % nfront) for f in range(nfront)]

    def x_ring(pieces):
        parts = [pieces[0]]
        for s in range(1, half_front):
            perm = [
                (h * half_front + i, h * half_front + (i + s) % half_front) for h in range(2) for i in range(half_front)
            ]
            parts.append(lax.ppermute(pieces[s], "front", perm))
        return parts

    def from_twin(mine):
        return lax.ppermute(lax.dynamic_index_in_dim(mine, 1 - hi, 0, keepdims=False), "front", twin)

    kids = child_blocks[0].reshape(slots * child_rows, width)
    kid_half = slots * child_rows // 2
    half = own_count // 2
    cut = half // 2
    kid_near = lax.ppermute(kids, "col", beside)
    own_near = lax.ppermute(own, "col", beside)
    got = [lax.ppermute(lax.dynamic_slice_in_dim(own, side * half, cut, 0), "col", across)]
    kid_send = lax.dynamic_slice_in_dim(child_blocks[0], side * (child_rows // 2), child_rows // 2, 1)
    got_kids = lax.ppermute(kid_send.reshape(kid_half, width), "col", across)

    kid_diag = kid_gram(ids, nfront, slots, kids, kids, kid_near, False, ids)
    got.append(lax.ppermute(far_rows(here, None, own, kid_diag, cut, half - cut), "col", across))
    rows = 1024
    own_diag = gram(ids, own, own, own_near, (1, own_count // rows), rows, lambda ids, b: 0, after=kid_diag)
    diag_pieces, _ = route(ids, slots, nfront, ring_send(kid_diag.reshape(slots * 2, width, width)), own_diag)
    own_sum = add_parts(ring_send(own_diag[0]), ids)
    kid_cross = kid_gram(ids, nfront, slots, got_kids, kids, kid_near, True, diag_pieces[1])
    cross_parts = ring_send(kid_cross.reshape(slots * 2, width, width))
    rows = 512
    half_at, cut_at = half // rows, cut // rows
    cross = gram(
        ids, got[0], own, own_near, (1, cut_at), rows, lambda ids, b: (1 - ids[1, 0] // 2) * half_at,
        after=own_sum,
    )
    diag_mine = add_parts(x_ring(diag_pieces), cross)
    cross_pieces, _ = route(ids, slots, nfront, cross_parts, diag_mine)
    cross = gram(
        ids, got[1], own, own_near, (1, half_at - cut_at), rows,
        lambda ids, b: (1 - ids[1, 0] // 2) * half_at + cut_at, flip=True, start=cross, after=diag_mine,
    )
    diag = diag_total(ids, half_front, own_sum, diag_mine, from_twin(diag_mine), cross)
    left = jnp.where(side == 0, diag, lax.ppermute(diag, "col", [(0, 2), (1, 3)]))
    cross_mine = add_parts(x_ring(cross_pieces), left)
    kid_cross_sum = lax.dynamic_index_in_dim(cross_mine, hi, 0, keepdims=False) + from_twin(cross_mine)

    quarters = cross[0].reshape(2, nrow, width // nrow, width)
    turns = []
    for s in range(nrow):
        piece = lax.dynamic_index_in_dim(quarters, (row_id + s) % nrow, 1, keepdims=False)
        piece = jnp.concatenate([piece, left])
        turns.append(piece if s == 0 else lax.ppermute(piece, "row", [(i, (i + s) % nrow) for i in range(nrow)]))
    cross = sum(turn[:2] for turn in turns)
    aa = jnp.stack([turn[2:] for turn in turns])
    aa_other = lax.ppermute(aa, "col", beside)

    cross = cross + kid_cross_sum
    same = lax.ppermute(cross[0], "col", [(0, 2), (1, 3)])
    swap = lax.ppermute(cross[1], "col", [(0, 3), (1, 2)])
    right = jnp.concatenate([cross + jnp.stack([same, swap]), diag])
    r_aa, m_aa = head(ids, aa, aa_other, right)
    right = joined(ring_gather(right), m_aa)
    out = tail(ids, r_aa, m_aa, right, lax.ppermute(right, "col", beside))
    return out[None]


def solution(mesh):
    in_specs = (P("front", "row", "col"), P("front", None, "row", "col"), P(), P(), P())
    out_specs = P("front", "row", "col")
    return jax.shard_map(shards, mesh=mesh, in_specs=in_specs, out_specs=out_specs, check_vma=False)
```
